128 devices in a mesh: group: 2 (over y_hi), tile: 64 (over x, z, y_lo, core).
Axes of the slice: x: 4, y: 4 (y_hi: 2, y_lo: 2; y = y_hi * 2 + y_lo), z: 4, core: 2. Of those that a mesh axis runs over, the one named last changes fastest.
Arguments:
- site_tensors: bfloat16 [64, 6, 2, 65536], P('tile', 'group'), may hold values from -6 to 6
- msg_in: float32 [64, 6, 4, 256], P('tile', 'group'), may hold values from -6 to 6
Outputs:
- new_tensors: bfloat16 [64, 6, 2, 65536], P('tile', 'group')
- messages: float32 [64, 6, 4, 256], P('tile', 'group')
The draws below stay inside these ranges and needn't reach their ends.
All inputs are finite; a program needn't handle non-finite values.
Results may differ from the reference program's by a relative error of at most 0.029.
The reference program's roundings to bfloat16 on the way count: a program that leaves them out, or rounds other values in their place, can miss the bound.
Values may be sent and summed in bfloat16 or wider, within the bound.
No kernel may reach another device: no remote copies, remote signals or barrier semaphores. Data moves between devices by JAX's collectives and lax.ppermute only.
A program may use at most 256 MiB of HBM per device.

```python
import math
import jax
import jax.numpy as jnp
from jax import lax

D = 16
ITERS = 2
NS_STEPS = 6
COLS = 6
ROWS = 64


def steps_of(own_key, extent, split, low, largest):
    def one(position, parts):
        draws = jax.random.uniform(jax.random.fold_in(jax.random.fold_in(own_key, 6), position), (parts,), jnp.float32, low / len(split), largest / len(split))
        return jnp.repeat(jnp.exp(draws), extent[position] // parts).reshape((-1,) + (1,) * (len(extent) - position - 1))

    factor_of = one(*split[0])
    for cut in split[1:]:
        factor_of = factor_of * one(*cut)
    return factor_of


def centred(key, extent, deviation, bound, cuts=(), kind=jnp.bfloat16):
    array = jax.random.normal(key, extent, jnp.float32) * deviation
    if len(cuts) > 0:
        array = steps_of(key, extent, cuts, -0.22, 0.18) * array
    return jnp.clip(array, min=-bound, max=bound).astype(kind)


def setup_inputs(seed: int = 0) -> dict:
    keys = jax.random.split(jax.random.key(seed), 3)
    site_tensors = centred(keys[0], (ROWS, COLS, 2, D**4), 1.0, 6.0, ((0, 64), (1, 2)))
    msg_in = centred(keys[1], (ROWS, COLS, 4, D*D), 1.0, 6.0, ((0, 64), (1, 2)), jnp.float32)
    return dict(site_tensors=site_tensors, msg_in=msg_in)


epsilon = 1e-06
coupling_step = 0.5
field_step = 0.3
precise = lax.Precision.HIGHEST
apply_forms = ('nsuldr,nua->nsaldr', 'nsuldr,nla->nsuadr', 'nsuldr,nda->nsular', 'nsuldr,nra->nsulda')
gate_forms = ('nsuldr,nsua->nsaldr', 'nsuldr,nsla->nsuadr', 'nsuldr,nsda->nsular', 'nsuldr,nsra->nsulda')
pair_forms = ('nsuldr,nsvldr->nsuv', 'nsuldr,nsuvdr->nslv', 'nsuldr,nsulvr->nsdv', 'nsuldr,nsuldv->nsrv')

def contract(form, left_op, right_op):
    return jnp.einsum(form, left_op.astype(jnp.float32), right_op.astype(jnp.float32), precision=precise)

def outgoing(tensors, incoming):
    site_count = tensors.shape[0]
    site_block = tensors.reshape(site_count, 2, D, D, D, D)
    msg_bf = incoming.reshape(site_count, 4, D, D).astype(jnp.bfloat16)

    def apply_leg(tensor, leg_idx):
        return contract(apply_forms[leg_idx], tensor, msg_bf[:, leg_idx]).astype(jnp.bfloat16)
    upper_left = apply_leg(apply_leg(site_block, 0), 1)
    lower_right = apply_leg(apply_leg(site_block, 2), 3)
    kept = (apply_leg(lower_right, 1), apply_leg(lower_right, 0), apply_leg(upper_left, 3), apply_leg(upper_left, 2))
    pairs = jnp.stack([contract(pair_forms[leg_idx], kept[leg_idx], site_block) for leg_idx in range(4)], axis=1)
    summed = pairs[:, :, 0] + pairs[:, :, 1]
    scale = jnp.sqrt(lax.optimization_barrier(jnp.mean(summed * summed, axis=(2, 3), keepdims=True)) + epsilon)
    twisted = (pairs[:, :, 0] - pairs[:, :, 1]) / scale
    return ((summed / scale).reshape(site_count, 4, D * D), twisted.reshape(site_count, 4, D * D))

def route(values, edge_msgs):
    in_up = jnp.concatenate([edge_msgs[:1, :, 0], values[:-1, :, 2]], axis=0)
    in_down = jnp.concatenate([values[1:, :, 0], edge_msgs[-1:, :, 2]], axis=0)
    in_left = jnp.concatenate([edge_msgs[:, :1, 1], values[:, :-1, 3]], axis=1)
    in_right = jnp.concatenate([values[:, 1:, 1], edge_msgs[:, -1:, 3]], axis=1)
    return jnp.stack([in_up, in_left, in_down, in_right], axis=2)

def leg_weights(msg_sum, twist_sum):
    weight_zero = math.cosh(coupling_step)
    weight_one = math.sinh(coupling_step)
    cross_weight = math.sqrt(weight_zero * weight_one)
    y_top = ((weight_zero * msg_sum + cross_weight * twist_sum) / math.sqrt(2.0)).astype(jnp.bfloat16).astype(jnp.float32)
    bottom = ((cross_weight * twist_sum + weight_one * msg_sum) / math.sqrt(2.0)).astype(jnp.bfloat16).astype(jnp.float32)
    gram_mat = jnp.einsum('...ab,...ac->...bc', y_top, y_top, precision=precise) + jnp.einsum('...ab,...ac->...bc', bottom, bottom, precision=precise)
    identity = jnp.eye(D, dtype=jnp.float32)
    trace_sum = lax.optimization_barrier(jnp.sum(gram_mat * identity, axis=(-2, -1), keepdims=True)) + epsilon
    current = gram_mat / trace_sum
    inverse = jnp.broadcast_to(identity, gram_mat.shape)
    for sweep in range(NS_STEPS):
        factor = 1.5 * identity - 0.5 * jnp.matmul(inverse, current, precision=precise)
        current, inverse = (jnp.matmul(current, factor, precision=precise), jnp.matmul(factor, inverse, precision=precise))
    inverse = inverse.astype(jnp.bfloat16).astype(jnp.float32)
    root_trace = jnp.sqrt(trace_sum)
    q_top = jnp.matmul(y_top, inverse, precision=precise) / root_trace
    q_bottom = jnp.matmul(bottom, inverse, precision=precise) / root_trace
    first = math.sqrt(weight_zero) * q_top
    second = math.sqrt(weight_one) * q_bottom
    return jnp.stack([first + second, first - second], axis=-3)

def update_row(tensors, weights):
    site_count = tensors.shape[0]
    site_block = tensors.reshape(site_count, 2, D, D, D, D).astype(jnp.float32)
    gated = (math.cosh(field_step) * site_block + math.sinh(field_step) * site_block[:, ::-1]).astype(jnp.bfloat16)
    for leg_idx in range(4):
        gated = contract(gate_forms[leg_idx], gated, weights[:, leg_idx]).astype(jnp.bfloat16)
    return gated.reshape(site_count, 2, D ** 4)

def reference(site_tensors, msg_in):
    incoming = msg_in
    for sweep in range(ITERS):
        summed, twisted = lax.map(lambda row_data: outgoing(row_data[0], row_data[1]), (site_tensors, incoming))
        incoming = route(summed, msg_in)
    twisted_in = route(twisted, jnp.zeros_like(msg_in))
    shape_env = (ROWS, COLS, 4, D, D)
    weights = leg_weights((summed + incoming).reshape(shape_env), (twisted + twisted_in).reshape(shape_env))
    row_ids = jnp.arange(ROWS)[:, None, None]
    col_ids = jnp.arange(COLS)[None, :, None]
    leg_ids = jnp.arange(4)[None, None, :]
    at_edge = (leg_ids == 0) & (row_ids == 0) | (leg_ids == 2) & (row_ids == ROWS - 1) | (leg_ids == 1) & (col_ids == 0) | (leg_ids == 3) & (col_ids == COLS - 1)
    identity = jnp.eye(D, dtype=jnp.float32)
    weights = jnp.where(at_edge[:, :, :, None, None, None], identity, weights).astype(jnp.bfloat16)
    new_tensors = lax.map(lambda row_data: update_row(row_data[0], row_data[1]), (site_tensors, weights))
    return (new_tensors, incoming)
```

```python
import math

import jax
import jax.numpy as jnp
from jax import lax
from jax.experimental import pallas as pl
from jax.experimental.pallas import tpu as pltpu
from jax.sharding import PartitionSpec as P

D = 16
SQ = D * D
SITES = 3
STATES = 2
ITERS = 2
NS_STEPS = 6
UP, LEFT, DOWN, RIGHT = range(4)
LEGS = (UP, DOWN, LEFT, RIGHT)

epsilon = 1e-06
coupling_step = 0.5
field_step = 0.3
f32 = jnp.float32
bf16 = jnp.bfloat16


def iota(shape, dim):
    return lax.broadcasted_iota(jnp.int32, shape, dim)


def where_ones(condition):
    return jnp.where(condition, 1.0, 0.0).astype(bf16)


def minor(index):
    return index & (D - 1)


def major(index):
    return index >> 4


def selector(row_part, lane_part):
    return where_ones(row_part(iota((SQ, SQ), 0)) == lane_part(iota((SQ, SQ), 1)))


def dot(left, right):
    return jnp.dot(left, right, preferred_element_type=f32)


def dot_split(left, right):
    high = left.astype(bf16)
    low = (left - high.astype(f32)).astype(bf16)
    return dot(high, right) + dot(low, right)


def masked_rows(rows, part):
    count = rows.shape[0]
    keep = iota((count, D, SQ), 1) == part(iota((count, D, SQ), 2))
    spread = jnp.broadcast_to(rows[:, None, :], (count, D, SQ))
    return jnp.where(keep, spread, 0.0).reshape(count * D, SQ)


def flat_rows(blocks):
    count = blocks.shape[0] // D
    keep = iota((count, D, SQ), 1) == major(iota((count, D, SQ), 2))
    return jnp.sum(jnp.where(keep, blocks.reshape(count, D, SQ), 0.0), axis=1)


def kron(rep, tile):
    return (rep.astype(f32)[:, None, :] * tile.astype(f32)[None, :, :]).astype(bf16).reshape(SQ, SQ)


def message_step(a_ref, at_ref, rows, split_states):
    count = SITES
    ends = masked_rows(jnp.concatenate([rows[UP], rows[DOWN]], axis=0), major).astype(bf16)
    sides = masked_rows(jnp.concatenate([rows[LEFT], rows[RIGHT]], axis=0), major).astype(bf16)
    rep = dot(ends, selector(minor, major)).reshape(2, count, D, SQ)
    tile = dot(sides, selector(minor, minor)).reshape(2, count, D, SQ)
    parts = {leg: [] for leg in LEGS}
    for site in range(count):
        up, down = rep[0, site], rep[1, site]
        left, right = tile[0, site], tile[1, site]
        for first, second, m_rep, m_tile, k_rep, k_tile, leg_rep, leg_tile in (
            (a_ref, at_ref, up, left, down, right, UP, LEFT),
            (at_ref, a_ref, down, right, up, left, DOWN, RIGHT),
        ):
            weight = kron(k_rep, k_tile)
            kept = [dot(first[site, s], weight).astype(bf16) for s in range(STATES)]
            products = [dot(kept[s], second[site, s]) for s in range(STATES)]
            if not split_states:
                products = [products[0] + products[1]]
            for product in products:
                cube = product.reshape(D, D, SQ)
                parts[leg_rep].append(jnp.sum(cube * m_tile[None, :, :], axis=1))
                parts[leg_tile].append(jnp.sum(cube * m_rep[:, None, :], axis=0))
    end_rows = flat_rows(
        dot_split(jnp.concatenate(parts[UP] + parts[DOWN], axis=0), selector(major, minor))
    )
    side_rows = flat_rows(
        dot_split(jnp.concatenate(parts[LEFT] + parts[RIGHT], axis=0), selector(minor, minor))
    )
    return jnp.concatenate([end_rows, side_rows], axis=0)


def scale_of(summed):
    return jnp.sqrt(jnp.mean(summed * summed, axis=1, keepdims=True) + epsilon)


def leg_rows(msg, leg):
    return jnp.concatenate([msg[site, leg : leg + 1] for site in range(SITES)], axis=0)


def group_of(leg):
    return LEGS.index(leg) * SITES


def pad_rows(parts):
    used = sum(part.shape[0] for part in parts)
    return jnp.concatenate(list(parts) + [jnp.zeros((8 - used, SQ), f32)], axis=0)


def place():
    tile = lax.axis_index("tile")
    return lax.axis_index("group"), tile, (tile & 1) == 0


def send(values, near_ref, far_ref, side_ref):
    group, _, even = place()
    ups = [value[0:3] for value in values]
    downs = [value[3:6] for value in values]
    near_ref[...] = jnp.where(even, pad_rows(downs), pad_rows(ups))
    far_ref[...] = jnp.where(even, pad_rows(ups), pad_rows(downs))
    side_ref[...] = jnp.where(
        group == 0,
        pad_rows([value[11:12] for value in values]),
        pad_rows([value[6:7] for value in values]),
    )


def receive(values, edges, near, far, side):
    group, tile, even = place()
    last = lax.axis_size("tile") - 1
    from_up = jnp.where(even, far, near)
    from_down = jnp.where(even, near, far)
    up = jnp.where(tile == 0, edges[UP], from_up)
    down = jnp.where(tile == last, edges[DOWN], from_down)
    left_end = jnp.where(group == 0, edges[LEFT][0:1], side)
    right_end = jnp.where(group == 0, side, edges[RIGHT][2:3])
    left = jnp.concatenate([left_end, values[9:11]], axis=0)
    right = jnp.concatenate([values[7:9], right_end], axis=0)
    return {UP: up, DOWN: down, LEFT: left, RIGHT: right}


def first_kernel(x_ref, msg_ref, a_ref, at_ref, out_ref, near_ref, far_ref, side_ref, wide_ref):
    eye = where_ones(iota((SQ, SQ), 0) == iota((SQ, SQ), 1))
    for site in range(SITES):
        wide_ref[...] = x_ref[site].astype(f32)
        for s in range(STATES):
            halves = [wide_ref[pl.ds(2 * half + s, SQ, stride=4), :] for half in range(2)]
            block = jnp.concatenate(halves, axis=1)
            a_ref[site, s] = block.astype(bf16)
            at_ref[site, s] = block.T.astype(bf16)
    msg = msg_ref[...]
    rows = {leg: leg_rows(msg, leg) for leg in LEGS}
    summed = message_step(a_ref, at_ref, rows, False)
    out = summed / scale_of(summed)
    out_ref[...] = out
    send([out], near_ref, far_ref, side_ref)


def second_kernel(
    a_ref, at_ref, msg_ref, old_ref, near_in, far_in, side_in,
    out_ref, twist_ref, near_ref, far_ref, side_ref,
):
    msg = msg_ref[...]
    edges = {leg: leg_rows(msg, leg) for leg in LEGS}
    rows = receive(old_ref[...], edges, near_in[0:3], far_in[0:3], side_in[0:1])
    pairs = message_step(a_ref, at_ref, rows, True)
    pairs = pairs.reshape(4 * SITES, STATES, SQ)
    summed = pairs[:, 0] + pairs[:, 1]
    scale = scale_of(summed)
    out = summed / scale
    twist = (pairs[:, 0] - pairs[:, 1]) / scale
    out_ref[...] = out
    twist_ref[...] = twist
    send([out, twist], near_ref, far_ref, side_ref)


def pack_product(lefts, rights):
    results = []
    for half in range(2):
        left = lefts[half]
        base = iota(left.shape, 1) & -D
        totals = [None] * len(rights)
        for k in range(D):
            column = jnp.take_along_axis(left, base + k, axis=1)
            for index, right in enumerate(rights):
                term = column * right[half][k : k + 1, :]
                totals[index] = term if totals[index] is None else totals[index] + term
        results.append(totals)
    return [[results[half][index] for half in range(2)] for index in range(len(rights))]


def halves_of(packed):
    return [packed[:, :128], packed[:, 128:]]


def on_diagonal(packed):
    spread = jnp.broadcast_to(packed[None], (D, D, SQ)).reshape(SQ, SQ)
    keep = major(iota((SQ, SQ), 0)) == major(iota((SQ, SQ), 1))
    return jnp.where(keep, spread, 0.0).astype(bf16)


def packed_of(diagonal):
    return jnp.sum(diagonal.reshape(D, D, SQ), axis=0)


def third_kernel(
    a_ref, msg_ref, old_ref, old_twist_ref, near_in, far_in, side_in, x_ref, messages_ref, wide_ref
):
    group, tile, _ = place()
    last = lax.axis_size("tile") - 1
    msg = msg_ref[...]
    edges = {leg: leg_rows(msg, leg) for leg in LEGS}
    zeros = {leg: jnp.zeros((SITES, SQ), f32) for leg in LEGS}
    old, old_twist = old_ref[...], old_twist_ref[...]
    incoming = receive(old, edges, near_in[0:3], far_in[0:3], side_in[0:1])
    twisted = receive(old_twist, zeros, near_in[3:6], far_in[3:6], side_in[1:2])
    for leg in LEGS:
        for site in range(SITES):
            messages_ref[site, leg : leg + 1] = incoming[leg][site : site + 1]
    fill = [jnp.zeros((4, SQ), f32)]
    both = jnp.concatenate([incoming[leg] for leg in LEGS], axis=0) + old
    both_twist = jnp.concatenate([twisted[leg] for leg in LEGS], axis=0) + old_twist
    both = jnp.concatenate([both] + fill, axis=0)
    both_twist = jnp.concatenate([both_twist] + fill, axis=0)

    weight_zero = math.cosh(coupling_step)
    weight_one = math.sinh(coupling_step)
    cross_weight = math.sqrt(weight_zero * weight_one)
    half_root = 1.0 / math.sqrt(2.0)
    top = ((weight_zero * both + cross_weight * both_twist) * half_root).astype(bf16).astype(f32)
    bottom = ((cross_weight * both_twist + weight_one * both) * half_root).astype(bf16).astype(f32)
    trace = jnp.sum(top * top + bottom * bottom, axis=1, keepdims=True) + epsilon
    own_lane = iota((D, SQ), 0) == major(iota((D, SQ), 1))
    trace = jnp.sum(jnp.where(own_lane, trace, 0.0), axis=0, keepdims=True)

    block = major(iota((SQ, SQ), 0)) == major(iota((SQ, SQ), 1))

    def diagonal(rows, part, other):
        spread = dot(masked_rows(rows, part).astype(bf16), selector(other, minor))
        return jnp.where(block, spread, 0.0)

    top_bd, bottom_bd = (diagonal(rows, major, minor) for rows in (top, bottom))
    top_t, bottom_t = (diagonal(rows, minor, major).astype(bf16) for rows in (top, bottom))
    gram = packed_of(dot(top_t, top_bd.astype(bf16)) + dot(bottom_t, bottom_bd.astype(bf16)))
    identity = jnp.where(iota((D, SQ), 0) == minor(iota((D, SQ), 1)), 1.0, 0.0)
    eye = halves_of(identity)
    current = halves_of(gram / trace)
    inverse = None
    for step in range(NS_STEPS):
        if inverse is None:
            product = current
        else:
            (product,) = pack_product(inverse, [current])
        factor = [1.5 * eye[half] - 0.5 * product[half] for half in range(2)]
        if inverse is None:
            (current,) = pack_product(factor, [current])
            inverse = factor
        elif step == NS_STEPS - 1:
            (inverse,) = pack_product(factor, [inverse])
        else:
            current, inverse = pack_product(factor, [current, inverse])
    inverse = jnp.concatenate(inverse, axis=1)
    inverse_bd = on_diagonal(inverse)
    root = jnp.sqrt(trace)
    q_pack = dot(
        jnp.concatenate([packed_of(top_bd), packed_of(bottom_bd)], axis=0).astype(bf16), inverse_bd
    )
    inverse_bf = inverse.astype(bf16)
    q_forms = (
        (q_pack[:D], q_pack[D:]),
        (dot(inverse_bf, top_t), dot(inverse_bf, bottom_t)),
    )
    row_group = major(iota((D, SQ), 1))
    at_edge = (
        ((row_group < 3) & (tile == 0))
        | ((row_group >= 3) & (row_group < 6) & (tile == last))
        | ((row_group == 6) & (group == 0))
        | ((row_group == 11) & (group == 1))
    )
    rep = selector(minor, major)
    tiled = selector(minor, minor)
    forms = []
    for q_top, q_bottom in q_forms:
        first = math.sqrt(weight_zero) * (q_top / root)
        second = math.sqrt(weight_one) * (q_bottom / root)
        per_state = []
        for weight in (first + second, first - second):
            weight = on_diagonal(jnp.where(at_edge, identity, weight))
            ends = dot(weight[: 6 * D], rep).reshape(6, D, SQ)
            sides = dot(weight[6 * D : 12 * D], tiled).reshape(6, D, SQ)
            per_state.append((ends, sides))
        forms.append(per_state)
    plain, flipped = forms
    grow, mix = math.cosh(field_step), math.sinh(field_step)
    for site in range(SITES):
        tensors = [a_ref[site, s].astype(f32) for s in range(STATES)]
        for s in range(STATES):
            gated = (grow * tensors[s] + mix * tensors[1 - s]).astype(bf16)
            upper = kron(flipped[s][0][site], flipped[s][1][site])
            lower = kron(plain[s][0][3 + site], plain[s][1][3 + site])
            gated = dot(upper, gated).astype(bf16)
            gated = dot(gated, lower)
            for half in range(2):
                wide_ref[pl.ds(2 * half + s, SQ, stride=4), :] = gated[:, half * 128 : half * 128 + 128]
        x_ref[site] = wide_ref[...].astype(bf16)


def call(kernel, outs, scratch=()):
    return pl.pallas_call(
        kernel,
        out_shape=[jax.ShapeDtypeStruct(shape, dtype) for shape, dtype in outs],
        scratch_shapes=list(scratch),
        compiler_params=pltpu.CompilerParams(vmem_limit_bytes=40 * 2**20),
    )


def swap_near(value):
    count = lax.axis_size("tile")
    return lax.ppermute(value, "tile", [(i, i ^ 1) for i in range(count)])


def swap_far(value):
    count = lax.axis_size("tile")
    return lax.ppermute(value, "tile", [(i, (((i + 1) ^ 1) - 1) % count) for i in range(count)])


def swap_side(value):
    return lax.ppermute(value, "group", [(0, 1), (1, 0)])


def exchange(near, far, side):
    return swap_near(near), swap_far(far), swap_side(side)


def per_device(site_tensors, msg_in):
    x = site_tensors.reshape(SITES, STATES, 2 * SQ, 128)
    x = x.transpose(0, 2, 1, 3).reshape(SITES, 4 * SQ, 128)
    msg = msg_in[0]
    tensor = ((SITES, STATES, SQ, SQ), bf16)
    rows = ((4 * SITES, SQ), f32)
    part = ((8, SQ), f32)
    wide = pltpu.VMEM((4 * SQ, 128), f32)
    a, at, out, *parts = call(first_kernel, [tensor, tensor, rows, part, part, part], [wide])(x, msg)
    parts = exchange(*parts)
    out, twist, *parts = call(second_kernel, [rows, rows, part, part, part])(a, at, msg, out, *parts)
    parts = exchange(*parts)
    x, messages = call(
        third_kernel, [((SITES, 4 * SQ, 128), bf16), ((SITES, 4, SQ), f32)], [wide]
    )(a, msg, out, twist, *parts)
    x = x.reshape(SITES, 2 * SQ, STATES, 128).transpose(0, 2, 1, 3)
    return x.reshape(1, SITES, STATES, SQ * SQ), messages[None]


def solution(mesh):
    spec = P("tile", "group", None, None)
    return jax.shard_map(
        per_device, mesh=mesh, in_specs=(spec, spec), out_specs=(spec, spec), check_vma=False
    )
```

```python
import math

import jax
import jax.numpy as jnp
from jax import lax
from jax.experimental import pallas as pl
from jax.experimental.pallas import tpu as pltpu
from jax.sharding import PartitionSpec as P

D = 16
SQ = D * D
SITES = 3
STATES = 2
ITERS = 2
NS_STEPS = 6
UP, LEFT, DOWN, RIGHT = range(4)
LEGS = (UP, DOWN, LEFT, RIGHT)
SLOTS = 8
WIDE = SLOTS * D

epsilon = 1e-06
coupling_step = 0.5
field_step = 0.3
f32 = jnp.float32
bf16 = jnp.bfloat16


def iota(shape, dim):
    return lax.broadcasted_iota(jnp.int32, shape, dim)


def where_ones(condition):
    return jnp.where(condition, 1.0, 0.0).astype(bf16)


def minor(index):
    return index & (D - 1)


def major(index):
    return index >> 4


def selector(row_part, lane_part, lanes):
    return where_ones(row_part(iota((SQ, lanes), 0)) == lane_part(iota((SQ, lanes), 1)))


def dot(left, right):
    return jnp.dot(left, right, preferred_element_type=f32)


def dot_first(left, right):
    return lax.dot_general(left, right, (((0,), (0,)), ((), ())), preferred_element_type=f32)


def dot_split(left, right):
    high = left.astype(bf16)
    low = (left - high.astype(f32)).astype(bf16)
    return dot(high, right) + dot(low, right)


def kron(rep, tile):
    return (rep.astype(f32)[:, None, :] * tile.astype(f32)[None, :, :]).astype(bf16).reshape(SQ, SQ)


def place():
    tile = lax.axis_index("tile")
    at_end = (tile == 0) | (tile == lax.axis_size("tile") - 1)
    return lax.axis_index("group") == 0, (tile & 1) == 0, at_end


def slot_of_lane():
    return major(iota((D, WIDE), 1))


def pack_of(blocks):
    slots = slot_of_lane()
    pack = jnp.zeros((D, WIDE), f32)
    for slot, block in enumerate(blocks):
        pack = jnp.where(slots == slot, block, pack)
    return pack


def packs_of(blocks):
    first_half, even, _ = place()
    near = [jnp.where(even, blocks[DOWN][i], blocks[UP][i]) for i in range(SITES)]
    far = [jnp.where(even, blocks[UP][i], blocks[DOWN][i]) for i in range(SITES)]
    side = jnp.where(first_half, blocks[RIGHT][2], blocks[LEFT][0])
    inner = [blocks[RIGHT][0], blocks[RIGHT][1], blocks[LEFT][1], blocks[LEFT][2]]
    return pack_of(near + inner), pack_of(far + [side])


def rep(pack, slot):
    lane = iota((D, WIDE), 1)
    return jnp.concatenate(
        [
            jnp.take_along_axis(pack, slot * D + half * SLOTS + major(lane), axis=1)
            for half in range(2)
        ],
        axis=1,
    )


def tile(pack, slot):
    part = jnp.take_along_axis(pack, slot * D + minor(iota((D, WIDE), 1)), axis=1)
    return jnp.concatenate([part, part], axis=1)


def site_parts(a_ref, at_ref, site, up, left, down, right, split_states):
    parts = {leg: [] for leg in LEGS}
    for first, second, m_rep, m_tile, k_rep, k_tile, leg_rep, leg_tile in (
        (a_ref, at_ref, up, left, down, right, UP, LEFT),
        (at_ref, a_ref, down, right, up, left, DOWN, RIGHT),
    ):
        weight = kron(k_rep, k_tile)
        kept = [dot(first[site, s], weight).astype(bf16) for s in range(STATES)]
        products = [dot(kept[s], second[site, s]) for s in range(STATES)]
        if not split_states:
            products = [products[0] + products[1]]
        for product in products:
            cube = product.reshape(D, D, SQ)
            parts[leg_rep].append(jnp.sum(cube * m_tile[None, :, :], axis=1))
            parts[leg_tile].append(jnp.sum(cube * m_rep[:, None, :], axis=0))
    return parts


def finish(parts, split_states):
    count = STATES if split_states else 1
    results = [{}, {}]
    for legs, pick in (
        ((UP, DOWN), selector(major, minor, WIDE)),
        ((LEFT, RIGHT), selector(minor, minor, WIDE)),
    ):
        rows = [parts[site][leg][s] for leg in legs for site in range(SITES) for s in range(count)]
        blocks = dot_split(jnp.concatenate(rows, axis=0), pick).reshape(2, SITES, count, D, WIDE)
        for index, leg in enumerate(legs):
            block = blocks[index]
            summed = block[:, 0] + block[:, 1] if split_states else block[:, 0]
            mean = jnp.mean(summed * summed, axis=(1, 2), keepdims=True)
            inverse = 1.0 / jnp.sqrt(mean + epsilon)
            results[0][leg] = summed * inverse
            if split_states:
                results[1][leg] = (block[:, 0] - block[:, 1]) * inverse
    return results


def leg_rows(msg, leg):
    return jnp.concatenate([msg[site, leg : leg + 1] for site in range(SITES)], axis=0)


def first_kernel(
    x_ref, msg_ref, a_ref, at_ref, edge_ref, near_ref, far_ref, x_buf, msg_buf, wide_ref, sems
):
    copies = [
        pltpu.make_async_copy(x_ref.at[site], x_buf.at[site], sems.at[site])
        for site in range(SITES)
    ]
    msg_copy = pltpu.make_async_copy(msg_ref, msg_buf, sems.at[SITES])
    msg_copy.start()
    for copy in copies:
        copy.start()
    msg_copy.wait()
    msg = msg_buf[...]
    rows = jnp.concatenate([leg_rows(msg, leg) for leg in LEGS], axis=0)
    count = rows.shape[0]
    keep = iota((count, D, SQ), 1) == major(iota((count, D, SQ), 2))
    spread = jnp.broadcast_to(rows[:, None, :], (count, D, SQ))
    spread = jnp.where(keep, spread, 0.0).reshape(count * D, SQ)
    ends = dot(spread[: count // 2 * D].astype(bf16), selector(minor, major, SQ))
    sides = dot(spread[count // 2 * D :].astype(bf16), selector(minor, minor, SQ))
    ends, sides = (both.reshape(2, SITES, D, SQ) for both in (ends, sides))
    exact = dot_split(spread, selector(minor, minor, WIDE)).reshape(4, SITES, D, WIDE)
    first_half, even, _ = place()
    outer = jnp.where(first_half, exact[2, 0], exact[3, 2])
    edges = [jnp.where(even, exact[0, i], exact[1, i]) for i in range(SITES)]
    edge_ref[...] = pack_of(edges + [outer])
    parts = []
    for site in range(SITES):
        copies[site].wait()
        wide_ref[site] = x_buf[site].astype(f32)
        for s in range(STATES):
            halves = [wide_ref[site, pl.ds(2 * half + s, SQ, stride=4), :] for half in range(2)]
            block = jnp.concatenate(halves, axis=1)
            a_ref[site, s] = block.astype(bf16)
            at_ref[site, s] = block.T.astype(bf16)
        parts.append(
            site_parts(
                a_ref, at_ref, site,
                ends[0, site], sides[0, site], ends[1, site], sides[1, site], False,
            )
        )
    out, _ = finish(parts, False)
    near_ref[...], far_ref[...] = packs_of(out)


def incoming_packs(near_own, edge, near_in, far_in, side_in):
    first_half, even, at_end = place()
    far = jnp.where(at_end, edge, far_in)
    up = jnp.where(even, far, near_in)
    down = jnp.where(even, near_in, far)
    left_end = jnp.where(first_half, edge, side_in)
    right_end = jnp.where(first_half, side_in, edge)
    return {
        UP: [(up, 0), (up, 1), (up, 2)],
        DOWN: [(down, 0), (down, 1), (down, 2)],
        LEFT: [(left_end, 3), (near_own, 3), (near_own, 4)],
        RIGHT: [(near_own, 5), (near_own, 6), (right_end, 3)],
    }


def second_kernel(
    a_ref, at_ref, edge_ref, near_own, near_in, far_in, side_in, near_ref, far_ref
):
    def rounded(ref):
        return ref[...].astype(bf16).astype(f32)

    where = incoming_packs(*(rounded(ref) for ref in (near_own, edge_ref, near_in, far_in, side_in)))
    parts = []
    for site in range(SITES):
        forms = [
            (rep if leg in (UP, DOWN) else tile)(*where[leg][site]) for leg in range(4)
        ]
        parts.append(site_parts(a_ref, at_ref, site, *forms, True))
    for index, values in enumerate(finish(parts, True)):
        near, far = packs_of(values)
        near_ref[index * D : index * D + D] = near
        far_ref[index * D : index * D + D] = far


def sum_of(terms):
    while len(terms) > 1:
        terms = [sum(terms[i : i + 2][1:], terms[i]) for i in range(0, len(terms), 2)]
    return terms[0]


def columns_of(pack):
    base = iota((D, WIDE), 1) & -D
    return [jnp.take_along_axis(pack, base + k, axis=1) for k in range(D)]


def times(columns, right):
    return sum_of([columns[k] * right[k : k + 1, :] for k in range(D)])


def inverse_root(power, eye):
    inverse = None
    for step in range(NS_STEPS):
        if inverse is None:
            following = 1.5 * eye - 0.5 * power
        columns = columns_of(power)
        if inverse is not None:
            following = 1.5 * inverse - 0.5 * times(columns, inverse)
        if step < NS_STEPS - 1:
            square = times(columns, power)
            power = 2.25 * power - 1.5 * square + 0.25 * times(columns, square)
        inverse = following
    return inverse


def bond_weights(both, both_twist, edge_lanes):
    weight_zero = math.cosh(coupling_step)
    weight_one = math.sinh(coupling_step)
    cross_weight = math.sqrt(weight_zero * weight_one)
    half_root = 1.0 / math.sqrt(2.0)
    top = ((weight_zero * both + cross_weight * both_twist) * half_root).astype(bf16).astype(f32)
    bottom = ((cross_weight * both_twist + weight_one * both) * half_root).astype(bf16).astype(f32)
    stacked = jnp.concatenate([top, bottom], axis=0).astype(bf16)
    inside = major(iota((WIDE, WIDE), 0)) == major(iota((WIDE, WIDE), 1))

    def packed(full):
        return jnp.sum(jnp.where(inside, full, 0.0).reshape(SLOTS, D, WIDE), axis=0)

    gram = packed(dot_first(stacked, stacked))
    squares = jnp.sum(top * top + bottom * bottom, axis=0, keepdims=True)
    squares = jnp.broadcast_to(squares, (D, WIDE))
    trace = dot_split(squares, where_ones(inside)) + epsilon
    identity = jnp.where(iota((D, WIDE), 0) == minor(iota((D, WIDE), 1)), 1.0, 0.0)
    inverse = inverse_root(gram / trace, identity).astype(bf16).astype(f32)
    spread = where_ones(iota((D, WIDE), 0) == minor(iota((D, WIDE), 1)))
    top_t, bottom_t = (packed(dot_first(half.astype(bf16), spread)) for half in (top, bottom))
    columns = columns_of(inverse)
    root = 1.0 / jnp.sqrt(trace)
    results = []
    for q_top, q_bottom in (
        (times(columns_of(top), inverse), times(columns_of(bottom), inverse)),
        (times(columns, top_t), times(columns, bottom_t)),
    ):
        first = math.sqrt(weight_zero) * (q_top * root)
        second = math.sqrt(weight_one) * (q_bottom * root)
        results.append(
            [
                jnp.where(edge_lanes, identity, weight).astype(bf16).astype(f32)
                for weight in (first + second, first - second)
            ]
        )
    return results


def early_kernel(a_ref, near_own, near_in, gated_ref, near_ref, inner_ref):
    _, even, _ = place()
    slots = slot_of_lane()
    other = (iota((D, WIDE), 1) + 2 * D) & (WIDE - 1)
    both = []
    for index in range(2):
        own = near_own[index * D : index * D + D]
        mate = jnp.take_along_axis(own, other, axis=1)
        mate = jnp.where(slots < 3, near_in[index * D : index * D + D], mate)
        both.append(jnp.where(slots < 5, own + mate, 0.0))
    grow, mix = math.cosh(field_step), math.sinh(field_step)
    for site in range(SITES):
        tensors = [a_ref[site, s].astype(f32) for s in range(STATES)]
        for s in range(STATES):
            gated_ref[site, s] = (grow * tensors[s] + mix * tensors[1 - s]).astype(bf16)
    plain, flipped = bond_weights(*both, slots < 0)
    for s in range(STATES):
        near = jnp.where(even, plain[s], flipped[s])
        for site in range(SITES):
            near_ref[s, site] = rep(near, site).astype(bf16)
        for index in range(2):
            inner_ref[s, 0, index] = tile(plain[s], 3 + index).astype(bf16)
            inner_ref[s, 1, index] = tile(flipped[s], 3 + index).astype(bf16)


def last_kernel(
    gated_ref, near_ref, inner_ref, edge_ref, near_own, far_own, near_in, far_in, side_in,
    x_ref, messages_ref, x_buf, msg_buf, wide_ref, sems,
):
    first_half, even, at_end = place()
    slots = slot_of_lane()
    both = []
    for index in range(2):
        part = slice(index * D, index * D + D)
        mate = jnp.where(slots < 3, far_in[part], side_in[part])
        both.append(jnp.where(slots < 4, far_own[part] + mate, 0.0))
    plain, flipped = bond_weights(*both, (slots < 3) & at_end)
    identity = where_ones(iota((D, SQ), 0) == minor(iota((D, SQ), 1)))
    factors = []
    for s in range(STATES):
        far_pack = jnp.where(even, flipped[s], plain[s])
        side = tile(jnp.where(first_half, plain[s], flipped[s]), 3).astype(bf16)
        far = [rep(far_pack, site).astype(bf16) for site in range(SITES)]
        near = [near_ref[s, site] for site in range(SITES)]
        ups = [jnp.where(even, far[i], near[i]) for i in range(SITES)]
        downs = [jnp.where(even, near[i], far[i]) for i in range(SITES)]
        lefts = [jnp.where(first_half, identity, side), inner_ref[s, 1, 0], inner_ref[s, 1, 1]]
        rights = [inner_ref[s, 0, 0], inner_ref[s, 0, 1], jnp.where(first_half, side, identity)]
        factors.append((ups, downs, lefts, rights))
    where = incoming_packs(
        near_own[:D], edge_ref[...], near_in[:D], far_in[:D], side_in[:D]
    )
    own_row = iota((D, SQ), 0) == major(iota((D, SQ), 1))
    for leg in LEGS:
        for site in range(SITES):
            spread = jnp.where(own_row, tile(*where[leg][site]), 0.0)
            msg_buf[site, leg : leg + 1] = jnp.sum(spread, axis=0, keepdims=True)
    msg_copy = pltpu.make_async_copy(msg_buf, messages_ref, sems.at[SITES])
    msg_copy.start()
    copies = []
    for site in range(SITES):
        for s in range(STATES):
            ups, downs, lefts, rights = factors[s]
            upper = kron(ups[site], lefts[site])
            lower = kron(downs[site], rights[site])
            gated = dot(upper, gated_ref[site, s]).astype(bf16)
            gated = dot(gated, lower)
            for half in range(2):
                lanes = gated[:, half * 128 : half * 128 + 128]
                wide_ref[site, pl.ds(2 * half + s, SQ, stride=4), :] = lanes
        x_buf[site] = wide_ref[site].astype(bf16)
        copies.append(pltpu.make_async_copy(x_buf.at[site], x_ref.at[site], sems.at[site]))
        copies[site].start()
    for copy in copies:
        copy.wait()
    msg_copy.wait()


def call(kernel, outs, scratch=(), in_specs=None, out_specs=None):
    specs = {}
    if in_specs is not None:
        specs["in_specs"] = in_specs
    if out_specs is not None:
        specs["out_specs"] = out_specs
    return pl.pallas_call(
        kernel,
        out_shape=[jax.ShapeDtypeStruct(shape, dtype) for shape, dtype in outs],
        scratch_shapes=list(scratch),
        compiler_params=pltpu.CompilerParams(vmem_limit_bytes=40 * 2**20),
        **specs,
    )


def swap_near(value):
    count = lax.axis_size("tile")
    return lax.ppermute(value, "tile", [(i, i ^ 1) for i in range(count)])


def swap_far(value):
    count = lax.axis_size("tile")
    return lax.ppermute(value, "tile", [(i, (((i + 1) ^ 1) - 1) % count) for i in range(count)])


def swap_side(value):
    return lax.ppermute(value, "group", [(0, 1), (1, 0)])


def exchange(near, far):
    return swap_near(near), swap_far(far), swap_side(far)


def per_device(site_tensors, msg_in):
    x = site_tensors.reshape(SITES, STATES, 2 * SQ, 128)
    x = x.transpose(0, 2, 1, 3).reshape(SITES, 4 * SQ, 128)
    x = pltpu.with_memory_space_constraint(x, pltpu.HBM)
    msg = pltpu.with_memory_space_constraint(msg_in[0], pltpu.HBM)
    flat = ((SITES, 4 * SQ, 128), bf16)
    tensor = ((SITES, STATES, SQ, SQ), bf16)
    messages = ((SITES, 4, SQ), f32)
    pack = ((D, WIDE), f32)
    packs = ((2 * D, WIDE), f32)
    in_hbm = [pl.BlockSpec(memory_space=pltpu.HBM)] * 2
    scratch = [
        pltpu.VMEM(*flat),
        pltpu.VMEM(*messages),
        pltpu.VMEM((SITES, 4 * SQ, 128), f32),
        pltpu.SemaphoreType.DMA((SITES + 1,)),
    ]
    a, at, edges, near, far = call(
        first_kernel, [tensor, tensor, pack, pack, pack], scratch, in_specs=in_hbm
    )(x, msg)
    near, far = call(second_kernel, [packs, packs])(a, at, edges, near, *exchange(near, far))
    received = exchange(near, far)
    spread = ((STATES, SITES, D, SQ), bf16)
    inner = ((STATES, 2, 2, D, SQ), bf16)
    early = call(early_kernel, [tensor, spread, inner])(a, near, received[0])
    x, messages = call(last_kernel, [flat, messages], scratch, out_specs=in_hbm)(
        *early, edges, near, far, *received
    )
    x = x.reshape(SITES, 2 * SQ, STATES, 128).transpose(0, 2, 1, 3)
    return x.reshape(1, SITES, STATES, SQ * SQ), messages[None]


def solution(mesh):
    spec = P("tile", "group", None, None)
    return jax.shard_map(
        per_device, mesh=mesh, in_specs=(spec, spec), out_specs=(spec, spec), check_vma=False
    )
```

```python
import math

import jax
import jax.numpy as jnp
from jax import lax
from jax.experimental import pallas as pl
from jax.experimental.pallas import tpu as pltpu
from jax.sharding import PartitionSpec as P

D = 16
SQ = D * D
SITES = 3
STATES = 2
ITERS = 2
NS_STEPS = 6
UP, LEFT, DOWN, RIGHT = range(4)
LEGS = (UP, DOWN, LEFT, RIGHT)
SLOTS = 8
WIDE = SLOTS * D

epsilon = 1e-06
coupling_step = 0.5
field_step = 0.3
f32 = jnp.float32
bf16 = jnp.bfloat16


def iota(shape, dim):
    return lax.broadcasted_iota(jnp.int32, shape, dim)


def where_ones(condition):
    return jnp.where(condition, 1.0, 0.0).astype(bf16)


def minor(index):
    return index & (D - 1)


def major(index):
    return index >> 4


def selector(row_part, lane_part, lanes):
    return where_ones(row_part(iota((SQ, lanes), 0)) == lane_part(iota((SQ, lanes), 1)))


def dot(left, right):
    return jnp.dot(left, right, preferred_element_type=f32)


def dot_first(left, right):
    return lax.dot_general(left, right, (((0,), (0,)), ((), ())), preferred_element_type=f32)


def dot_split(left, right):
    high = left.astype(bf16)
    low = (left - high.astype(f32)).astype(bf16)
    return dot(high, right) + dot(low, right)


def kron(rep, tile):
    return (rep.astype(f32)[:, None, :] * tile.astype(f32)[None, :, :]).astype(bf16).reshape(SQ, SQ)


def place():
    tile = lax.axis_index("tile")
    at_end = (tile == 0) | (tile == lax.axis_size("tile") - 1)
    return lax.axis_index("group") == 0, (tile & 1) == 0, at_end


def slot_of_lane():
    return major(iota((D, WIDE), 1))


def pack_of(blocks):
    slots = slot_of_lane()
    pack = jnp.zeros((D, WIDE), f32)
    for slot, block in enumerate(blocks):
        pack = jnp.where(slots == slot, block, pack)
    return pack


def packs_of(blocks):
    first_half, even, _ = place()
    near = [jnp.where(even, blocks[DOWN][i], blocks[UP][i]) for i in range(SITES)]
    far = [jnp.where(even, blocks[UP][i], blocks[DOWN][i]) for i in range(SITES)]
    side = jnp.where(first_half, blocks[RIGHT][2], blocks[LEFT][0])
    inner = [blocks[RIGHT][0], blocks[RIGHT][1], blocks[LEFT][1], blocks[LEFT][2]]
    return pack_of(near + inner), pack_of(far + [side])


def rep(pack, slot):
    lane = iota((D, WIDE), 1)
    return jnp.concatenate(
        [
            jnp.take_along_axis(pack, slot * D + half * SLOTS + major(lane), axis=1)
            for half in range(2)
        ],
        axis=1,
    )


def tile(pack, slot):
    part = jnp.take_along_axis(pack, slot * D + minor(iota((D, WIDE), 1)), axis=1)
    return jnp.concatenate([part, part], axis=1)


def site_parts(a_ref, at_ref, site, up, left, down, right, split_states):
    parts = {leg: [] for leg in LEGS}
    for first, second, m_rep, m_tile, k_rep, k_tile, leg_rep, leg_tile in (
        (a_ref, at_ref, up, left, down, right, UP, LEFT),
        (at_ref, a_ref, down, right, up, left, DOWN, RIGHT),
    ):
        weight = kron(k_rep, k_tile)
        kept = [dot(first[site, s], weight).astype(bf16) for s in range(STATES)]
        products = [dot(kept[s], second[site, s]) for s in range(STATES)]
        if not split_states:
            products = [products[0] + products[1]]
        for product in products:
            cube = product.reshape(D, D, SQ)
            parts[leg_rep].append(jnp.sum(cube * m_tile[None, :, :], axis=1))
            parts[leg_tile].append(jnp.sum(cube * m_rep[:, None, :], axis=0))
    return parts


def finish(parts, split_states):
    count = STATES if split_states else 1
    results = [{}, {}]
    for legs, pick in (
        ((UP, DOWN), selector(major, minor, WIDE)),
        ((LEFT, RIGHT), selector(minor, minor, WIDE)),
    ):
        rows = [parts[site][leg][s] for leg in legs for site in range(SITES) for s in range(count)]
        blocks = dot_split(jnp.concatenate(rows, axis=0), pick).reshape(2, SITES, count, D, WIDE)
        for index, leg in enumerate(legs):
            block = blocks[index]
            summed = block[:, 0] + block[:, 1] if split_states else block[:, 0]
            mean = jnp.mean(summed * summed, axis=(1, 2), keepdims=True)
            inverse = 1.0 / jnp.sqrt(mean + epsilon)
            results[0][leg] = summed * inverse
            if split_states:
                results[1][leg] = (block[:, 0] - block[:, 1]) * inverse
    return results


def leg_rows(msg, leg):
    return jnp.concatenate([msg[site, leg : leg + 1] for site in range(SITES)], axis=0)


def first_kernel(
    x_ref, msg_ref, a_ref, at_ref, edge_ref, own_ref, near_ref, far_ref, side_ref,
    x_buf, msg_buf, wide_ref, sems,
):
    copies = [
        pltpu.make_async_copy(x_ref.at[site], x_buf.at[site], sems.at[site])
        for site in range(SITES)
    ]
    msg_copy = pltpu.make_async_copy(msg_ref, msg_buf, sems.at[SITES])
    msg_copy.start()
    for copy in copies:
        copy.start()
    msg_copy.wait()
    msg = msg_buf[...]
    rows = jnp.concatenate([leg_rows(msg, leg) for leg in LEGS], axis=0)
    count = rows.shape[0]
    keep = iota((count, D, SQ), 1) == major(iota((count, D, SQ), 2))
    spread = jnp.broadcast_to(rows[:, None, :], (count, D, SQ))
    spread = jnp.where(keep, spread, 0.0).reshape(count * D, SQ)
    ends = dot(spread[: count // 2 * D].astype(bf16), selector(minor, major, SQ))
    sides = dot(spread[count // 2 * D :].astype(bf16), selector(minor, minor, SQ))
    ends, sides = (both.reshape(2, SITES, D, SQ) for both in (ends, sides))
    exact = dot_split(spread, selector(minor, minor, WIDE)).reshape(4, SITES, D, WIDE)
    first_half, even, _ = place()
    outer = jnp.where(first_half, exact[2, 0], exact[3, 2])
    edges = [jnp.where(even, exact[0, i], exact[1, i]) for i in range(SITES)]
    edge_ref[...] = pack_of(edges + [outer])
    parts = []
    for copy in copies:
        copy.wait()
    for site in range(SITES):
        wide_ref[site] = x_buf[site].astype(f32)
        for s in range(STATES):
            halves = [wide_ref[site, pl.ds(2 * half + s, SQ, stride=4), :] for half in range(2)]
            block = jnp.concatenate(halves, axis=1)
            a_ref[site, s] = block.astype(bf16)
            at_ref[site, s] = block.T.astype(bf16)
        parts.append(
            site_parts(
                a_ref, at_ref, site,
                ends[0, site], sides[0, site], ends[1, site], sides[1, site], False,
            )
        )
    out, _ = finish(parts, False)
    near, far = packs_of(out)
    own_ref[...] = near
    near_ref[...] = near
    far_ref[...] = far
    side_ref[...] = far


def incoming_packs(near_own, edge, near_in, far_in, side_in):
    first_half, even, at_end = place()
    far = jnp.where(at_end, edge, far_in)
    up = jnp.where(even, far, near_in)
    down = jnp.where(even, near_in, far)
    left_end = jnp.where(first_half, edge, side_in)
    right_end = jnp.where(first_half, side_in, edge)
    return {
        UP: [(up, 0), (up, 1), (up, 2)],
        DOWN: [(down, 0), (down, 1), (down, 2)],
        LEFT: [(left_end, 3), (near_own, 3), (near_own, 4)],
        RIGHT: [(near_own, 5), (near_own, 6), (right_end, 3)],
    }


def second_kernel(
    a_ref, at_ref, edge_ref, near_own, near_in, far_in, side_in,
    own_near_ref, own_far_ref, near_ref, far_ref, side_ref,
):
    def rounded(ref):
        return ref[...].astype(bf16).astype(f32)

    where = incoming_packs(*(rounded(ref) for ref in (near_own, edge_ref, near_in, far_in, side_in)))
    parts = []
    for site in range(SITES):
        forms = [
            (rep if leg in (UP, DOWN) else tile)(*where[leg][site]) for leg in range(4)
        ]
        parts.append(site_parts(a_ref, at_ref, site, *forms, True))
    for index, values in enumerate(finish(parts, True)):
        near, far = packs_of(values)
        part = slice(index * D, index * D + D)
        own_near_ref[part] = near
        own_far_ref[part] = far
        near_ref[part] = near
        far_ref[part] = far
        side_ref[part] = far


def sum_of(terms):
    while len(terms) > 1:
        terms = [sum(terms[i : i + 2][1:], terms[i]) for i in range(0, len(terms), 2)]
    return terms[0]


def columns_of(pack):
    base = iota((D, WIDE), 1) & -D
    return [jnp.take_along_axis(pack, base + k, axis=1) for k in range(D)]


def times(columns, right):
    return sum_of([columns[k] * right[k : k + 1, :] for k in range(D)])


def inverse_root(power, eye):
    inverse = None
    for step in range(NS_STEPS):
        if inverse is None:
            following = 1.5 * eye - 0.5 * power
        columns = columns_of(power)
        if inverse is not None:
            following = 1.5 * inverse - 0.5 * times(columns, inverse)
        if step < NS_STEPS - 1:
            square = times(columns, power)
            power = 2.25 * power - 1.5 * square + 0.25 * times(columns, square)
        inverse = following
    return inverse


def bond_weights(both, both_twist, edge_lanes):
    weight_zero = math.cosh(coupling_step)
    weight_one = math.sinh(coupling_step)
    cross_weight = math.sqrt(weight_zero * weight_one)
    half_root = 1.0 / math.sqrt(2.0)
    top = ((weight_zero * both + cross_weight * both_twist) * half_root).astype(bf16).astype(f32)
    bottom = ((cross_weight * both_twist + weight_one * both) * half_root).astype(bf16).astype(f32)
    stacked = jnp.concatenate([top, bottom], axis=0).astype(bf16)
    inside = major(iota((WIDE, WIDE), 0)) == major(iota((WIDE, WIDE), 1))

    def packed(full):
        return jnp.sum(jnp.where(inside, full, 0.0).reshape(SLOTS, D, WIDE), axis=0)

    gram = packed(dot_first(stacked, stacked))
    squares = jnp.sum(top * top + bottom * bottom, axis=0, keepdims=True)
    squares = jnp.broadcast_to(squares, (D, WIDE))
    trace = dot_split(squares, where_ones(inside)) + epsilon
    identity = jnp.where(iota((D, WIDE), 0) == minor(iota((D, WIDE), 1)), 1.0, 0.0)
    inverse = inverse_root(gram / trace, identity).astype(bf16).astype(f32)
    spread = where_ones(iota((D, WIDE), 0) == minor(iota((D, WIDE), 1)))
    top_t, bottom_t = (packed(dot_first(half.astype(bf16), spread)) for half in (top, bottom))
    columns = columns_of(inverse)
    root = 1.0 / jnp.sqrt(trace)
    results = []
    for q_top, q_bottom in (
        (times(columns_of(top), inverse), times(columns_of(bottom), inverse)),
        (times(columns, top_t), times(columns, bottom_t)),
    ):
        first = math.sqrt(weight_zero) * (q_top * root)
        second = math.sqrt(weight_one) * (q_bottom * root)
        results.append(
            [
                jnp.where(edge_lanes, identity, weight).astype(bf16).astype(f32)
                for weight in (first + second, first - second)
            ]
        )
    return results


def early_kernel(a_ref, near_own, near_in, gated_ref, near_ref, inner_ref):
    _, even, _ = place()
    slots = slot_of_lane()
    other = (iota((D, WIDE), 1) + 2 * D) & (WIDE - 1)
    both = []
    for index in range(2):
        own = near_own[index * D : index * D + D]
        mate = jnp.take_along_axis(own, other, axis=1)
        mate = jnp.where(slots < 3, near_in[index * D : index * D + D], mate)
        both.append(jnp.where(slots < 5, own + mate, 0.0))
    grow, mix = math.cosh(field_step), math.sinh(field_step)
    for site in range(SITES):
        tensors = [a_ref[site, s].astype(f32) for s in range(STATES)]
        for s in range(STATES):
            gated_ref[site, s] = (grow * tensors[s] + mix * tensors[1 - s]).astype(bf16)
    plain, flipped = bond_weights(*both, slots < 0)
    for s in range(STATES):
        near = jnp.where(even, plain[s], flipped[s])
        for site in range(SITES):
            near_ref[s, site] = rep(near, site).astype(bf16)
        for index in range(2):
            inner_ref[s, 0, index] = tile(plain[s], 3 + index).astype(bf16)
            inner_ref[s, 1, index] = tile(flipped[s], 3 + index).astype(bf16)


def last_kernel(
    gated_ref, near_ref, inner_ref, edge_ref, near_own, far_own, near_in, far_in, side_in,
    x_ref, messages_ref, x_buf, msg_buf, wide_ref, sems,
):
    first_half, even, at_end = place()
    slots = slot_of_lane()
    both = []
    for index in range(2):
        part = slice(index * D, index * D + D)
        mate = jnp.where(slots < 3, far_in[part], side_in[part])
        both.append(jnp.where(slots < 4, far_own[part] + mate, 0.0))
    plain, flipped = bond_weights(*both, (slots < 3) & at_end)
    identity = where_ones(iota((D, SQ), 0) == minor(iota((D, SQ), 1)))
    factors = []
    for s in range(STATES):
        far_pack = jnp.where(even, flipped[s], plain[s])
        side = tile(jnp.where(first_half, plain[s], flipped[s]), 3).astype(bf16)
        far = [rep(far_pack, site).astype(bf16) for site in range(SITES)]
        near = [near_ref[s, site] for site in range(SITES)]
        ups = [jnp.where(even, far[i], near[i]) for i in range(SITES)]
        downs = [jnp.where(even, near[i], far[i]) for i in range(SITES)]
        lefts = [jnp.where(first_half, identity, side), inner_ref[s, 1, 0], inner_ref[s, 1, 1]]
        rights = [inner_ref[s, 0, 0], inner_ref[s, 0, 1], jnp.where(first_half, side, identity)]
        factors.append((ups, downs, lefts, rights))
    where = incoming_packs(
        near_own[:D], edge_ref[...], near_in[:D], far_in[:D], side_in[:D]
    )
    own_row = iota((D, SQ), 0) == major(iota((D, SQ), 1))
    for leg in LEGS:
        for site in range(SITES):
            spread = jnp.where(own_row, tile(*where[leg][site]), 0.0)
            msg_buf[site, leg : leg + 1] = jnp.sum(spread, axis=0, keepdims=True)
    msg_copy = pltpu.make_async_copy(msg_buf, messages_ref, sems.at[SITES])
    msg_copy.start()
    copies = []
    for site in range(SITES):
        for s in range(STATES):
            ups, downs, lefts, rights = factors[s]
            upper = kron(ups[site], lefts[site])
            lower = kron(downs[site], rights[site])
            gated = dot(upper, gated_ref[site, s]).astype(bf16)
            gated = dot(gated, lower)
            for half in range(2):
                lanes = gated[:, half * 128 : half * 128 + 128]
                wide_ref[site, pl.ds(2 * half + s, SQ, stride=4), :] = lanes
        x_buf[site] = wide_ref[site].astype(bf16)
        copies.append(pltpu.make_async_copy(x_buf.at[site], x_ref.at[site], sems.at[site]))
        copies[site].start()
    for copy in copies:
        copy.wait()
    msg_copy.wait()


def call(kernel, outs, scratch=(), in_specs=None, out_specs=None):
    specs = {}
    if in_specs is not None:
        specs["in_specs"] = in_specs
    if out_specs is not None:
        specs["out_specs"] = out_specs
    return pl.pallas_call(
        kernel,
        out_shape=[jax.ShapeDtypeStruct(shape, dtype) for shape, dtype in outs],
        scratch_shapes=list(scratch),
        compiler_params=pltpu.CompilerParams(vmem_limit_bytes=40 * 2**20),
        **specs,
    )


def swap_near(value):
    count = lax.axis_size("tile")
    return lax.ppermute(value, "tile", [(i, i ^ 1) for i in range(count)])


def swap_far(value):
    count = lax.axis_size("tile")
    return lax.ppermute(value, "tile", [(i, (((i + 1) ^ 1) - 1) % count) for i in range(count)])


def swap_side(value):
    return lax.ppermute(value, "group", [(0, 1), (1, 0)])


def exchange(near, far, side):
    return swap_near(near), swap_far(far), swap_side(side)


def per_device(site_tensors, msg_in):
    x = site_tensors.reshape(SITES, STATES, 2 * SQ, 128)
    x = x.transpose(0, 2, 1, 3).reshape(SITES, 4 * SQ, 128)
    x = pltpu.with_memory_space_constraint(x, pltpu.HBM)
    msg = pltpu.with_memory_space_constraint(msg_in[0], pltpu.HBM)
    flat = ((SITES, 4 * SQ, 128), bf16)
    tensor = ((SITES, STATES, SQ, SQ), bf16)
    messages = ((SITES, 4, SQ), f32)
    pack = ((D, WIDE), f32)
    packs = ((2 * D, WIDE), f32)
    in_hbm = [pl.BlockSpec(memory_space=pltpu.HBM)] * 2
    scratch = [
        pltpu.VMEM(*flat),
        pltpu.VMEM(*messages),
        pltpu.VMEM((SITES, 4 * SQ, 128), f32),
        pltpu.SemaphoreType.DMA((SITES + 1,)),
    ]
    a, at, edges, own, *parts = call(
        first_kernel, [tensor, tensor, pack, pack, pack, pack, pack], scratch, in_specs=in_hbm
    )(x, msg)
    near, far, *parts = call(second_kernel, [packs] * 5)(a, at, edges, own, *exchange(*parts))
    received = exchange(*parts)
    spread = ((STATES, SITES, D, SQ), bf16)
    inner = ((STATES, 2, 2, D, SQ), bf16)
    early = call(early_kernel, [tensor, spread, inner])(a, near, received[0])
    x, messages = call(last_kernel, [flat, messages], scratch, out_specs=in_hbm)(
        *early, edges, near, far, *received
    )
    x = x.reshape(SITES, 2 * SQ, STATES, 128).transpose(0, 2, 1, 3)
    return x.reshape(1, SITES, STATES, SQ * SQ), messages[None]


def solution(mesh):
    spec = P("tile", "group", None, None)
    return jax.shard_map(
        per_device, mesh=mesh, in_specs=(spec, spec), out_specs=(spec, spec), check_vma=False
    )
```

```python
import math

import jax
import jax.numpy as jnp
from jax import lax
from jax.experimental import pallas as pl
from jax.experimental.pallas import tpu as pltpu
from jax.sharding import PartitionSpec as P

D = 16
SQ = D * D
SITES = 3
STATES = 2
ITERS = 2
NS_STEPS = 6
UP, LEFT, DOWN, RIGHT = range(4)
LEGS = (UP, DOWN, LEFT, RIGHT)
SLOTS = 8
WIDE = SLOTS * D

epsilon = 1e-06
coupling_step = 0.5
field_step = 0.3
f32 = jnp.float32
bf16 = jnp.bfloat16


def iota(shape, dim):
    return lax.broadcasted_iota(jnp.int32, shape, dim)


def where_ones(condition):
    return jnp.where(condition, 1.0, 0.0).astype(bf16)


def minor(index):
    return index & (D - 1)


def major(index):
    return index >> 4


def selector(row_part, lane_part, lanes):
    return where_ones(row_part(iota((SQ, lanes), 0)) == lane_part(iota((SQ, lanes), 1)))


def dot(left, right):
    return jnp.dot(left, right, preferred_element_type=f32)


def dot_first(left, right):
    return lax.dot_general(left, right, (((0,), (0,)), ((), ())), preferred_element_type=f32)


def dot_split(left, right):
    high = left.astype(bf16)
    low = (left - high.astype(f32)).astype(bf16)
    return dot(high, right) + dot(low, right)


def kron(rep, tile):
    return (rep.astype(f32)[:, None, :] * tile.astype(f32)[None, :, :]).astype(bf16).reshape(SQ, SQ)


def place():
    tile = lax.axis_index("tile")
    at_end = (tile == 0) | (tile == lax.axis_size("tile") - 1)
    return lax.axis_index("group") == 0, (tile & 1) == 0, at_end


def slot_of_lane():
    return major(iota((D, WIDE), 1))


def pack_of(blocks):
    slots = slot_of_lane()
    pack = jnp.zeros((D, WIDE), f32)
    for slot, block in enumerate(blocks):
        pack = jnp.where(slots == slot, block, pack)
    return pack


def packs_of(blocks):
    first_half, even, _ = place()
    near = [jnp.where(even, blocks[DOWN][i], blocks[UP][i]) for i in range(SITES)]
    far = [jnp.where(even, blocks[UP][i], blocks[DOWN][i]) for i in range(SITES)]
    side = jnp.where(first_half, blocks[RIGHT][2], blocks[LEFT][0])
    inner = [blocks[RIGHT][0], blocks[RIGHT][1], blocks[LEFT][1], blocks[LEFT][2]]
    return pack_of(near + inner), pack_of(far + [side])


def rep(pack, slot):
    lane = iota((D, WIDE), 1)
    return jnp.concatenate(
        [
            jnp.take_along_axis(pack, slot * D + half * SLOTS + major(lane), axis=1)
            for half in range(2)
        ],
        axis=1,
    )


def tile(pack, slot):
    part = jnp.take_along_axis(pack, slot * D + minor(iota((D, WIDE), 1)), axis=1)
    return jnp.concatenate([part, part], axis=1)


def site_parts(a_ref, at_ref, site, up, left, down, right, split_states):
    parts = {leg: [] for leg in LEGS}
    for first, second, m_rep, m_tile, k_rep, k_tile, leg_rep, leg_tile in (
        (a_ref, at_ref, up, left, down, right, UP, LEFT),
        (at_ref, a_ref, down, right, up, left, DOWN, RIGHT),
    ):
        weight = kron(k_rep, k_tile)
        kept = [dot(first[site, s], weight).astype(bf16) for s in range(STATES)]
        products = [dot(kept[s], second[site, s]) for s in range(STATES)]
        if not split_states:
            products = [products[0] + products[1]]
        for product in products:
            cube = product.reshape(D, D, SQ)
            parts[leg_rep].append(jnp.sum(cube * m_tile[None, :, :], axis=1))
            parts[leg_tile].append(jnp.sum(cube * m_rep[:, None, :], axis=0))
    return parts


def finish(parts, split_states):
    count = STATES if split_states else 1
    results = [{}, {}]
    for legs, pick in (
        ((UP, DOWN), selector(major, minor, WIDE)),
        ((LEFT, RIGHT), selector(minor, minor, WIDE)),
    ):
        rows = [parts[site][leg][s] for leg in legs for site in range(SITES) for s in range(count)]
        blocks = dot_split(jnp.concatenate(rows, axis=0), pick).reshape(2, SITES, count, D, WIDE)
        for index, leg in enumerate(legs):
            block = blocks[index]
            summed = block[:, 0] + block[:, 1] if split_states else block[:, 0]
            mean = jnp.mean(summed * summed, axis=(1, 2), keepdims=True)
            inverse = 1.0 / jnp.sqrt(mean + epsilon)
            results[0][leg] = summed * inverse
            if split_states:
                results[1][leg] = (block[:, 0] - block[:, 1]) * inverse
    return results


def leg_rows(msg, leg):
    return jnp.concatenate([msg[site, leg : leg + 1] for site in range(SITES)], axis=0)


def first_kernel(
    x_ref, msg_ref, a_ref, at_ref, edge_ref, own_ref, near_ref, far_ref, side_ref,
    x_buf, msg_buf, wide_ref, sems,
):
    copies = [
        pltpu.make_async_copy(x_ref.at[site], x_buf.at[site], sems.at[site])
        for site in range(SITES)
    ]
    msg_copy = pltpu.make_async_copy(msg_ref, msg_buf, sems.at[SITES])
    msg_copy.start()
    for copy in copies:
        copy.start()
    msg_copy.wait()
    msg = msg_buf[...]
    rows = jnp.concatenate([leg_rows(msg, leg) for leg in LEGS], axis=0)
    count = rows.shape[0]
    keep = iota((count, D, SQ), 1) == major(iota((count, D, SQ), 2))
    spread = jnp.broadcast_to(rows[:, None, :], (count, D, SQ))
    spread = jnp.where(keep, spread, 0.0).reshape(count * D, SQ)
    ends = dot(spread[: count // 2 * D].astype(bf16), selector(minor, major, SQ))
    sides = dot(spread[count // 2 * D :].astype(bf16), selector(minor, minor, SQ))
    ends, sides = (both.reshape(2, SITES, D, SQ) for both in (ends, sides))
    exact = dot_split(spread, selector(minor, minor, WIDE)).reshape(4, SITES, D, WIDE)
    first_half, even, _ = place()
    outer = jnp.where(first_half, exact[2, 0], exact[3, 2])
    edges = [jnp.where(even, exact[0, i], exact[1, i]) for i in range(SITES)]
    edge_ref[...] = pack_of(edges + [outer])
    parts = []
    for copy in copies:
        copy.wait()
    for site in range(SITES):
        wide_ref[site] = x_buf[site].astype(f32)
        for s in range(STATES):
            halves = [wide_ref[site, pl.ds(2 * half + s, SQ, stride=4), :] for half in range(2)]
            block = jnp.concatenate(halves, axis=1)
            a_ref[site, s] = block.astype(bf16)
            at_ref[site, s] = block.T.astype(bf16)
        parts.append(
            site_parts(
                a_ref, at_ref, site,
                ends[0, site], sides[0, site], ends[1, site], sides[1, site], False,
            )
        )
    out, _ = finish(parts, False)
    near, far = packs_of(out)
    own_ref[...] = near
    near_ref[...] = near
    far_ref[...] = far
    side_ref[...] = far


def incoming_packs(near_own, edge, near_in, far_in, side_in):
    first_half, even, at_end = place()
    far = jnp.where(at_end, edge, far_in)
    up = jnp.where(even, far, near_in)
    down = jnp.where(even, near_in, far)
    left_end = jnp.where(first_half, edge, side_in)
    right_end = jnp.where(first_half, side_in, edge)
    return {
        UP: [(up, 0), (up, 1), (up, 2)],
        DOWN: [(down, 0), (down, 1), (down, 2)],
        LEFT: [(left_end, 3), (near_own, 3), (near_own, 4)],
        RIGHT: [(near_own, 5), (near_own, 6), (right_end, 3)],
    }


def second_kernel(
    a_ref, at_ref, edge_ref, near_own, near_in, far_in, side_in,
    own_near_ref, own_far_ref, near_ref, far_ref, side_ref,
):
    def rounded(ref):
        return ref[...].astype(bf16).astype(f32)

    where = incoming_packs(*(rounded(ref) for ref in (near_own, edge_ref, near_in, far_in, side_in)))
    parts = []
    for site in range(SITES):
        forms = [
            (rep if leg in (UP, DOWN) else tile)(*where[leg][site]) for leg in range(4)
        ]
        parts.append(site_parts(a_ref, at_ref, site, *forms, True))
    for index, values in enumerate(finish(parts, True)):
        near, far = packs_of(values)
        part = slice(index * D, index * D + D)
        own_near_ref[part] = near
        own_far_ref[part] = far
        near_ref[part] = near
        far_ref[part] = far
        side_ref[part] = far


def sum_of(terms):
    while len(terms) > 1:
        terms = [sum(terms[i : i + 2][1:], terms[i]) for i in range(0, len(terms), 2)]
    return terms[0]


def columns_of(pack):
    base = iota((D, WIDE), 1) & -D
    return [jnp.take_along_axis(pack, base + k, axis=1) for k in range(D)]


def times(columns, right):
    return sum_of([columns[k] * right[k : k + 1, :] for k in range(D)])


def inverse_root(power, eye):
    inverse = None
    for step in range(NS_STEPS):
        if inverse is None:
            following = 1.5 * eye - 0.5 * power
        columns = columns_of(power)
        if inverse is not None:
            following = 1.5 * inverse - 0.5 * times(columns, inverse)
        if step < NS_STEPS - 1:
            square = times(columns, power)
            power = 2.25 * power - 1.5 * square + 0.25 * times(columns, square)
        inverse = following
    return inverse


def bond_weights(both, both_twist, edge_lanes):
    weight_zero = math.cosh(coupling_step)
    weight_one = math.sinh(coupling_step)
    cross_weight = math.sqrt(weight_zero * weight_one)
    half_root = 1.0 / math.sqrt(2.0)
    top = ((weight_zero * both + cross_weight * both_twist) * half_root).astype(bf16).astype(f32)
    bottom = ((cross_weight * both_twist + weight_one * both) * half_root).astype(bf16).astype(f32)
    stacked = jnp.concatenate([top, bottom], axis=0).astype(bf16)
    inside = major(iota((WIDE, WIDE), 0)) == major(iota((WIDE, WIDE), 1))

    def packed(full):
        return jnp.sum(jnp.where(inside, full, 0.0).reshape(SLOTS, D, WIDE), axis=0)

    gram = packed(dot_first(stacked, stacked))
    squares = jnp.sum(top * top + bottom * bottom, axis=0, keepdims=True)
    squares = jnp.broadcast_to(squares, (D, WIDE))
    trace = dot_split(squares, where_ones(inside)) + epsilon
    identity = jnp.where(iota((D, WIDE), 0) == minor(iota((D, WIDE), 1)), 1.0, 0.0)
    inverse = inverse_root(gram / trace, identity).astype(bf16).astype(f32)
    spread = where_ones(iota((D, WIDE), 0) == minor(iota((D, WIDE), 1)))
    top_t, bottom_t = (packed(dot_first(half.astype(bf16), spread)) for half in (top, bottom))
    columns = columns_of(inverse)
    root = 1.0 / jnp.sqrt(trace)
    results = []
    for q_top, q_bottom in (
        (times(columns_of(top), inverse), times(columns_of(bottom), inverse)),
        (times(columns, top_t), times(columns, bottom_t)),
    ):
        first = math.sqrt(weight_zero) * (q_top * root)
        second = math.sqrt(weight_one) * (q_bottom * root)
        results.append(
            [
                jnp.where(edge_lanes, identity, weight).astype(bf16).astype(f32)
                for weight in (first + second, first - second)
            ]
        )
    return results


def early_kernel(a_ref, near_own, near_in, gated_ref, near_ref, inner_ref):
    _, even, _ = place()
    slots = slot_of_lane()
    other = (iota((D, WIDE), 1) + 2 * D) & (WIDE - 1)
    both = []
    for index in range(2):
        own = near_own[index * D : index * D + D]
        mate = jnp.take_along_axis(own, other, axis=1)
        mate = jnp.where(slots < 3, near_in[index * D : index * D + D], mate)
        both.append(jnp.where(slots < 5, own + mate, 0.0))
    grow, mix = math.cosh(field_step), math.sinh(field_step)
    for site in range(SITES):
        tensors = [a_ref[site, s].astype(f32) for s in range(STATES)]
        for s in range(STATES):
            gated_ref[site, s] = (grow * tensors[s] + mix * tensors[1 - s]).astype(bf16)
    plain, flipped = bond_weights(*both, slots < 0)
    for s in range(STATES):
        near = jnp.where(even, plain[s], flipped[s])
        for site in range(SITES):
            near_ref[s, site] = rep(near, site).astype(bf16)
        for index in range(2):
            inner_ref[s, 0, index] = tile(plain[s], 3 + index).astype(bf16)
            inner_ref[s, 1, index] = tile(flipped[s], 3 + index).astype(bf16)


def last_kernel(
    gated_ref, near_ref, inner_ref, edge_ref, near_own, far_own, near_in, far_in, side_in,
    x_ref, messages_ref, x_buf, msg_buf, wide_ref, sems,
):
    first_half, even, at_end = place()
    slots = slot_of_lane()
    both = []
    for index in range(2):
        part = slice(index * D, index * D + D)
        mate = jnp.where(slots < 3, far_in[part], side_in[part])
        both.append(jnp.where(slots < 4, far_own[part] + mate, 0.0))
    plain, flipped = bond_weights(*both, (slots < 3) & at_end)
    identity = where_ones(iota((D, SQ), 0) == minor(iota((D, SQ), 1)))
    factors = []
    for s in range(STATES):
        far_pack = jnp.where(even, flipped[s], plain[s])
        side = tile(jnp.where(first_half, plain[s], flipped[s]), 3).astype(bf16)
        far = [rep(far_pack, site).astype(bf16) for site in range(SITES)]
        near = [near_ref[s, site] for site in range(SITES)]
        ups = [jnp.where(even, far[i], near[i]) for i in range(SITES)]
        downs = [jnp.where(even, near[i], far[i]) for i in range(SITES)]
        lefts = [jnp.where(first_half, identity, side), inner_ref[s, 1, 0], inner_ref[s, 1, 1]]
        rights = [inner_ref[s, 0, 0], inner_ref[s, 0, 1], jnp.where(first_half, side, identity)]
        factors.append((ups, downs, lefts, rights))
    where = incoming_packs(
        near_own[:D], edge_ref[...], near_in[:D], far_in[:D], side_in[:D]
    )
    own_row = iota((D, SQ), 0) == major(iota((D, SQ), 1))
    for leg in LEGS:
        for site in range(SITES):
            spread = jnp.where(own_row, tile(*where[leg][site]), 0.0)
            msg_buf[site, leg : leg + 1] = jnp.sum(spread, axis=0, keepdims=True)
    msg_copy = pltpu.make_async_copy(msg_buf, messages_ref, sems.at[SITES])
    msg_copy.start()
    copies = []
    for site in range(SITES):
        for s in range(STATES):
            ups, downs, lefts, rights = factors[s]
            upper = kron(ups[site], lefts[site])
            lower = kron(downs[site], rights[site])
            gated = dot(upper, gated_ref[site, s]).astype(bf16)
            gated = dot(gated, lower)
            for half in range(2):
                lanes = gated[:, half * 128 : half * 128 + 128]
                wide_ref[site, pl.ds(2 * half + s, SQ, stride=4), :] = lanes
        x_buf[site] = wide_ref[site].astype(bf16)
        copies.append(pltpu.make_async_copy(x_buf.at[site], x_ref.at[site], sems.at[site]))
        copies[site].start()
    for copy in copies:
        copy.wait()
    msg_copy.wait()


def call(kernel, outs, scratch=(), in_specs=None, out_specs=None):
    specs = {}
    if in_specs is not None:
        specs["in_specs"] = in_specs
    if out_specs is not None:
        specs["out_specs"] = out_specs
    return pl.pallas_call(
        kernel,
        out_shape=[jax.ShapeDtypeStruct(shape, dtype) for shape, dtype in outs],
        scratch_shapes=list(scratch),
        compiler_params=pltpu.CompilerParams(vmem_limit_bytes=40 * 2**20),
        **specs,
    )


def swap_near(value):
    count = lax.axis_size("tile")
    return lax.ppermute(value, "tile", [(i, i ^ 1) for i in range(count)])


def swap_far(value):
    count = lax.axis_size("tile")
    pairs = []
    for group in range(2):
        for i in range(count):
            other = ((i + 1) ^ 1) - 1
            inner = 0 <= other < count
            target = group * count + other if inner else (1 - group) * count + i
            pairs.append((group * count + i, target))
    return lax.ppermute(value, ("group", "tile"), pairs)


def swap_side(value):
    return lax.ppermute(value, "group", [(0, 1), (1, 0)])


def exchange(near, far, side):
    return swap_near(near), swap_far(far), swap_side(side)


def per_device(site_tensors, msg_in):
    x = site_tensors.reshape(SITES, STATES, 2 * SQ, 128)
    x = x.transpose(0, 2, 1, 3).reshape(SITES, 4 * SQ, 128)
    x = pltpu.with_memory_space_constraint(x, pltpu.HBM)
    msg = pltpu.with_memory_space_constraint(msg_in[0], pltpu.HBM)
    flat = ((SITES, 4 * SQ, 128), bf16)
    tensor = ((SITES, STATES, SQ, SQ), bf16)
    messages = ((SITES, 4, SQ), f32)
    pack = ((D, WIDE), f32)
    packs = ((2 * D, WIDE), f32)
    in_hbm = [pl.BlockSpec(memory_space=pltpu.HBM)] * 2
    scratch = [
        pltpu.VMEM(*flat),
        pltpu.VMEM(*messages),
        pltpu.VMEM((SITES, 4 * SQ, 128), f32),
        pltpu.SemaphoreType.DMA((SITES + 1,)),
    ]
    a, at, edges, own, *parts = call(
        first_kernel, [tensor, tensor, pack, pack, pack, pack, pack], scratch, in_specs=in_hbm
    )(x, msg)
    near, far, *parts = call(second_kernel, [packs] * 5)(a, at, edges, own, *exchange(*parts))
    received = exchange(*parts)
    spread = ((STATES, SITES, D, SQ), bf16)
    inner = ((STATES, 2, 2, D, SQ), bf16)
    early = call(early_kernel, [tensor, spread, inner])(a, near, received[0])
    x, messages = call(last_kernel, [flat, messages], scratch, out_specs=in_hbm)(
        *early, edges, near, far, *received
    )
    x = x.reshape(SITES, 2 * SQ, STATES, 128).transpose(0, 2, 1, 3)
    return x.reshape(1, SITES, STATES, SQ * SQ), messages[None]


def solution(mesh):
    spec = P("tile", "group", None, None)
    return jax.shard_map(
        per_device, mesh=mesh, in_specs=(spec, spec), out_specs=(spec, spec), check_vma=False
    )
```

```python
import math

import jax
import jax.numpy as jnp
from jax import lax
from jax.experimental import pallas as pl
from jax.experimental.pallas import tpu as pltpu
from jax.sharding import PartitionSpec as P

D = 16
SQ = D * D
SITES = 3
STATES = 2
ITERS = 2
NS_STEPS = 6
UP, LEFT, DOWN, RIGHT = range(4)
LEGS = (UP, DOWN, LEFT, RIGHT)
SLOTS = 8
WIDE = SLOTS * D

epsilon = 1e-06
coupling_step = 0.5
field_step = 0.3
f32 = jnp.float32
bf16 = jnp.bfloat16


def iota(shape, dim):
    return lax.broadcasted_iota(jnp.int32, shape, dim)


def where_ones(condition):
    return jnp.where(condition, 1.0, 0.0).astype(bf16)


def minor(index):
    return index & (D - 1)


def major(index):
    return index >> 4


def selector(row_part, lane_part, lanes):
    return where_ones(row_part(iota((SQ, lanes), 0)) == lane_part(iota((SQ, lanes), 1)))


def dot(left, right):
    return jnp.dot(left, right, preferred_element_type=f32)


def dot_first(left, right):
    return lax.dot_general(left, right, (((0,), (0,)), ((), ())), preferred_element_type=f32)


def dot_split(left, right):
    high = left.astype(bf16)
    low = (left - high.astype(f32)).astype(bf16)
    return dot(high, right) + dot(low, right)


def kron(rep, tile):
    return (rep.astype(bf16)[:, None, :] * tile.astype(bf16)[None, :, :]).reshape(SQ, SQ)


def place():
    tile = lax.axis_index("tile")
    at_end = (tile == 0) | (tile == lax.axis_size("tile") - 1)
    return lax.axis_index("group") == 0, (tile & 1) == 0, at_end


def slot_of_lane():
    return major(iota((D, WIDE), 1))


def pack_of(blocks):
    slots = slot_of_lane()
    pack = jnp.zeros((D, WIDE), f32)
    for slot, block in enumerate(blocks):
        pack = jnp.where(slots == slot, block, pack)
    return pack


def packs_of(near, far, left, right):
    first_half, _, _ = place()
    side = jnp.where(first_half, right[2], left[0])
    inner = [right[0], right[1], left[1], left[2]]
    return pack_of(near + inner), pack_of(far + [side])


def rep(pack, slot):
    lane = iota((D, WIDE), 1)
    return jnp.concatenate(
        [
            jnp.take_along_axis(pack, slot * D + half * SLOTS + major(lane), axis=1)
            for half in range(2)
        ],
        axis=1,
    )


def tile(pack, slot):
    part = jnp.take_along_axis(pack, slot * D + minor(iota((D, WIDE), 1)), axis=1)
    return jnp.concatenate([part, part], axis=1)


def product(x_ref, form, site, s, weight):
    kept = dot(x_ref[form, site, s], weight).astype(bf16)
    return dot(kept, x_ref[1 - form, site, s])


def fold_minor(full, form):
    return jnp.sum(full.reshape(D, D, SQ) * form[None, :, :], axis=1)


def fold_major(full, form):
    return jnp.sum(full.reshape(D, D, SQ) * form[:, None, :], axis=0)


def site_parts(x_ref, site, up, left, down, right):
    parts = {}
    for form, m_rep, m_tile, k_rep, k_tile, leg_rep, leg_tile in (
        (0, up, left, down, right, UP, LEFT),
        (1, down, right, up, left, DOWN, RIGHT),
    ):
        weight = kron(k_rep, k_tile)
        full = product(x_ref, form, site, 0, weight) + product(x_ref, form, site, 1, weight)
        parts[leg_rep] = [fold_minor(full, m_tile)]
        parts[leg_tile] = [fold_major(full, m_rep)]
    return parts


def finish(parts, split_states):
    count = STATES if split_states else 1
    results = [{}, {}]
    for legs, pick in (
        ((UP, DOWN), selector(major, minor, WIDE)),
        ((LEFT, RIGHT), selector(minor, minor, WIDE)),
    ):
        rows = [parts[site][leg][s] for leg in legs for site in range(SITES) for s in range(count)]
        blocks = dot(jnp.concatenate(rows, axis=0).astype(bf16), pick).reshape(2, SITES, count, D, WIDE)
        for index, leg in enumerate(legs):
            block = blocks[index]
            summed = block[:, 0] + block[:, 1] if split_states else block[:, 0]
            mean = jnp.mean(summed * summed, axis=(1, 2), keepdims=True)
            inverse = 1.0 / jnp.sqrt(mean + epsilon)
            results[0][leg] = summed * inverse
            if split_states:
                results[1][leg] = (block[:, 0] - block[:, 1]) * inverse
    return results


def leg_rows(msg, leg):
    return jnp.concatenate([msg[site, leg : leg + 1] for site in range(SITES)], axis=0)


def first_kernel(
    x_ref, msg_ref, form_ref, edge_ref, own_ref, near_ref, far_ref, side_ref,
    x_buf, msg_buf, wide_ref, sems,
):
    copies = [
        pltpu.make_async_copy(x_ref.at[site], x_buf.at[site], sems.at[site])
        for site in range(SITES)
    ]
    msg_copy = pltpu.make_async_copy(msg_ref, msg_buf, sems.at[SITES])
    msg_copy.start()
    for copy in copies:
        copy.start()
    msg_copy.wait()
    msg = msg_buf[...]
    rows = jnp.concatenate([leg_rows(msg, leg) for leg in LEGS], axis=0)
    count = rows.shape[0]
    keep = iota((count, D, SQ), 1) == major(iota((count, D, SQ), 2))
    spread = jnp.broadcast_to(rows[:, None, :], (count, D, SQ))
    spread = jnp.where(keep, spread, 0.0).reshape(count * D, SQ)
    ends = dot(spread[: count // 2 * D].astype(bf16), selector(minor, major, SQ))
    sides = dot(spread[count // 2 * D :].astype(bf16), selector(minor, minor, SQ))
    ends, sides = (both.reshape(2, SITES, D, SQ) for both in (ends, sides))
    exact = dot_split(spread, selector(minor, minor, WIDE)).reshape(4, SITES, D, WIDE)
    first_half, even, _ = place()
    outer = jnp.where(first_half, exact[2, 0], exact[3, 2])
    edges = [jnp.where(even, exact[0, i], exact[1, i]) for i in range(SITES)]
    edge_ref[...] = pack_of(edges + [outer])
    parts = []
    for copy in copies:
        copy.wait()
    for site in range(SITES):
        wide_ref[site] = x_buf[site].astype(f32)
        for s in range(STATES):
            halves = [wide_ref[site, pl.ds(2 * half + s, SQ, stride=4), :] for half in range(2)]
            block = jnp.concatenate(halves, axis=1)
            form_ref[0, site, s] = block.astype(bf16)
            form_ref[1, site, s] = block.T.astype(bf16)
        parts.append(
            site_parts(form_ref, site, ends[0, site], sides[0, site], ends[1, site], sides[1, site])
        )
    out, _ = finish(parts, False)
    near = [jnp.where(even, out[DOWN][i], out[UP][i]) for i in range(SITES)]
    far = [jnp.where(even, out[UP][i], out[DOWN][i]) for i in range(SITES)]
    near, far = packs_of(near, far, out[LEFT], out[RIGHT])
    own_ref[...] = near
    near_ref[...] = near
    far_ref[...] = far
    side_ref[...] = far


def incoming_packs(near_own, edge, near_in, far_in, side_in):
    first_half, even, at_end = place()
    far = jnp.where(at_end, edge, far_in)
    up = jnp.where(even, far, near_in)
    down = jnp.where(even, near_in, far)
    left_end = jnp.where(first_half, edge, side_in)
    right_end = jnp.where(first_half, side_in, edge)
    return {
        UP: [(up, 0), (up, 1), (up, 2)],
        DOWN: [(down, 0), (down, 1), (down, 2)],
        LEFT: [(left_end, 3), (near_own, 3), (near_own, 4)],
        RIGHT: [(near_own, 5), (near_own, 6), (right_end, 3)],
    }


def site_forms(near, edge, own, far=None, side=None):
    first_half, even, _ = place()

    def pick(one, two):
        return jnp.where(first_half, one, two)

    sites = [1, pick(0, 2), pick(2, 0)]
    outer, near_side = tile(edge, 3), None if side is None else tile(side, 3)
    sides = [
        (tile(own, 3), tile(own, 6)),
        (pick(outer, tile(own, 4)), pick(tile(own, 5), outer)),
    ]
    if side is not None:
        sides.append((pick(tile(own, 4), near_side), pick(near_side, tile(own, 5))))
    forms = []
    for index, (left, right) in enumerate(sides):
        ends = []
        for pack in (near, far):
            if pack is None:
                ends.append(None)
            elif index == 0:
                ends.append(rep(pack, 1))
            else:
                zero, two = rep(pack, 0), rep(pack, 2)
                ends.append(pick(zero, two) if index == 1 else pick(two, zero))
        forms.append((sites[index], *ends, jnp.where(even, right, left), jnp.where(even, left, right)))
    return forms


def rounded(ref):
    return ref[...].astype(bf16).astype(f32)


def parity():
    return lax.axis_index("tile") & 1


def ahead_kernel(form_ref, edge_ref, near_own, near_in, full_ref, part_ref):
    form = parity()
    forms = site_forms(rounded(near_in), rounded(edge_ref), rounded(near_own))
    for index, (site, near, _, with_near, with_far) in enumerate(forms):
        weight = kron(near, with_near)
        for s in range(STATES):
            full = product(form_ref, form, site, s, weight)
            full_ref[index, s] = full
            part_ref[index, s] = fold_minor(full, with_far)


def second_kernel(
    form_ref, edge_ref, near_own, near_in, far_in, side_in, full_ref, part_ref,
    own_near_ref, own_far_ref, near_ref, far_ref, side_ref,
):
    first_half, even, at_end = place()
    form = parity()
    edge = rounded(edge_ref)
    far = jnp.where(at_end, edge, rounded(far_in))
    forms = site_forms(rounded(near_in), edge, rounded(near_own), far, rounded(side_in))
    parts = []
    for index, (site, near, far, with_near, with_far) in enumerate(forms):
        legs = {leg: [] for leg in LEGS}
        ahead, behind = kron(near, with_near), kron(far, with_far)
        for s in range(STATES):
            if index < 2:
                full, part = full_ref[index, s], part_ref[index, s]
            else:
                full = product(form_ref, form, site, s, ahead)
                part = fold_minor(full, with_far)
            legs[UP].append(part)
            legs[LEFT].append(fold_major(full, far))
            full = product(form_ref, 1 - form, site, s, behind)
            legs[DOWN].append(fold_minor(full, with_near))
            legs[RIGHT].append(fold_major(full, near))
        parts.append(legs)

    def by_site(values):
        middle, outer, inner = values
        return [jnp.where(first_half, outer, inner), middle, jnp.where(first_half, inner, outer)]

    for index, values in enumerate(finish(parts, True)):
        near, far, with_far, with_near = (
            by_site([values[leg][i] for i in range(SITES)]) for leg in (DOWN, UP, LEFT, RIGHT)
        )
        left = [jnp.where(even, with_far[i], with_near[i]) for i in range(SITES)]
        right = [jnp.where(even, with_near[i], with_far[i]) for i in range(SITES)]
        near, far = packs_of(near, far, left, right)
        part = slice(index * D, index * D + D)
        own_near_ref[part] = near
        own_far_ref[part] = far
        near_ref[part] = near
        far_ref[part] = far
        side_ref[part] = far


def sum_of(terms):
    while len(terms) > 1:
        terms = [sum(terms[i : i + 2][1:], terms[i]) for i in range(0, len(terms), 2)]
    return terms[0]


def columns_of(pack):
    base = iota((D, WIDE), 1) & -D
    return [jnp.take_along_axis(pack, base + k, axis=1) for k in range(D)]


def times(columns, right):
    return sum_of([columns[k] * right[k : k + 1, :] for k in range(D)])


def inverse_root(power, eye):
    inverse = None
    for step in range(NS_STEPS):
        if inverse is None:
            following = 1.5 * eye - 0.5 * power
        columns = columns_of(power)
        if inverse is not None:
            following = 1.5 * inverse - 0.5 * times(columns, inverse)
        if step < NS_STEPS - 1:
            square = times(columns, power)
            power = 2.25 * power - 1.5 * square + 0.25 * times(columns, square)
        inverse = following
    return inverse


def bond_weights(both, both_twist, edge_lanes):
    weight_zero = math.cosh(coupling_step)
    weight_one = math.sinh(coupling_step)
    cross_weight = math.sqrt(weight_zero * weight_one)
    half_root = 1.0 / math.sqrt(2.0)
    top = ((weight_zero * both + cross_weight * both_twist) * half_root).astype(bf16).astype(f32)
    bottom = ((cross_weight * both_twist + weight_one * both) * half_root).astype(bf16).astype(f32)
    stacked = jnp.concatenate([top, bottom], axis=0).astype(bf16)
    inside = major(iota((WIDE, WIDE), 0)) == major(iota((WIDE, WIDE), 1))

    def packed(full):
        return jnp.sum(jnp.where(inside, full, 0.0).reshape(SLOTS, D, WIDE), axis=0)

    gram = packed(dot_first(stacked, stacked))
    squares = jnp.sum(top * top + bottom * bottom, axis=0, keepdims=True)
    squares = jnp.broadcast_to(squares, (D, WIDE))
    trace = dot_split(squares, where_ones(inside)) + epsilon
    identity = jnp.where(iota((D, WIDE), 0) == minor(iota((D, WIDE), 1)), 1.0, 0.0)
    inverse = inverse_root(gram / trace, identity).astype(bf16).astype(f32)
    spread = where_ones(iota((D, WIDE), 0) == minor(iota((D, WIDE), 1)))
    top_t, bottom_t = (packed(dot_first(half.astype(bf16), spread)) for half in (top, bottom))
    columns = columns_of(inverse)
    root = 1.0 / jnp.sqrt(trace)
    results = []
    for q_top, q_bottom in (
        (times(columns_of(top), inverse), times(columns_of(bottom), inverse)),
        (times(columns, top_t), times(columns, bottom_t)),
    ):
        first = math.sqrt(weight_zero) * (q_top * root)
        second = math.sqrt(weight_one) * (q_bottom * root)
        results.append(
            [
                jnp.where(edge_lanes, identity, weight).astype(bf16).astype(f32)
                for weight in (first + second, first - second)
            ]
        )
    return results


def early_kernel(form_ref, near_own, near_in, gated_ref, near_ref, inner_ref):
    _, even, _ = place()
    slots = slot_of_lane()
    other = (iota((D, WIDE), 1) + 2 * D) & (WIDE - 1)
    both = []
    for index in range(2):
        own = near_own[index * D : index * D + D]
        mate = jnp.take_along_axis(own, other, axis=1)
        mate = jnp.where(slots < 3, near_in[index * D : index * D + D], mate)
        both.append(jnp.where(slots < 5, own + mate, 0.0))
    grow, mix = math.cosh(field_step), math.sinh(field_step)
    for site in range(SITES):
        tensors = [form_ref[0, site, s].astype(f32) for s in range(STATES)]
        for s in range(STATES):
            gated_ref[site, s] = (grow * tensors[s] + mix * tensors[1 - s]).astype(bf16)
    plain, flipped = bond_weights(*both, slots < 0)
    for s in range(STATES):
        near = jnp.where(even, plain[s], flipped[s])
        for site in range(SITES):
            near_ref[s, site] = rep(near, site).astype(bf16)
        for index in range(2):
            inner_ref[s, 0, index] = tile(plain[s], 3 + index).astype(bf16)
            inner_ref[s, 1, index] = tile(flipped[s], 3 + index).astype(bf16)


def last_kernel(
    gated_ref, near_ref, inner_ref, edge_ref, near_own, far_own, near_in, far_in, side_in,
    x_ref, messages_ref, x_buf, msg_buf, wide_ref, sems,
):
    first_half, even, at_end = place()
    slots = slot_of_lane()
    where = incoming_packs(
        near_own[:D], edge_ref[...], near_in[:D], far_in[:D], side_in[:D]
    )
    own_row = iota((D, SQ), 0) == major(iota((D, SQ), 1))
    for leg in LEGS:
        for site in range(SITES):
            spread = jnp.where(own_row, tile(*where[leg][site]), 0.0)
            msg_buf[site, leg : leg + 1] = jnp.sum(spread, axis=0, keepdims=True)
    msg_copy = pltpu.make_async_copy(msg_buf, messages_ref, sems.at[SITES])
    msg_copy.start()
    both = []
    for index in range(2):
        part = slice(index * D, index * D + D)
        mate = jnp.where(slots < 3, far_in[part], side_in[part])
        both.append(jnp.where(slots < 4, far_own[part] + mate, 0.0))
    plain, flipped = bond_weights(*both, (slots < 3) & at_end)
    identity = where_ones(iota((D, SQ), 0) == minor(iota((D, SQ), 1)))
    factors = []
    for s in range(STATES):
        far_pack = jnp.where(even, flipped[s], plain[s])
        side = tile(jnp.where(first_half, plain[s], flipped[s]), 3).astype(bf16)
        far = [rep(far_pack, site).astype(bf16) for site in range(SITES)]
        near = [near_ref[s, site] for site in range(SITES)]
        ups = [jnp.where(even, far[i], near[i]) for i in range(SITES)]
        downs = [jnp.where(even, near[i], far[i]) for i in range(SITES)]
        lefts = [jnp.where(first_half, identity, side), inner_ref[s, 1, 0], inner_ref[s, 1, 1]]
        rights = [inner_ref[s, 0, 0], inner_ref[s, 0, 1], jnp.where(first_half, side, identity)]
        factors.append((ups, downs, lefts, rights))
    copies = []
    for site in range(SITES):
        for s in range(STATES):
            ups, downs, lefts, rights = factors[s]
            upper = kron(ups[site], lefts[site])
            lower = kron(downs[site], rights[site])
            gated = dot(upper, gated_ref[site, s]).astype(bf16)
            gated = dot(gated, lower)
            for half in range(2):
                lanes = gated[:, half * 128 : half * 128 + 128]
                wide_ref[site, pl.ds(2 * half + s, SQ, stride=4), :] = lanes
        x_buf[site] = wide_ref[site].astype(bf16)
        copies.append(pltpu.make_async_copy(x_buf.at[site], x_ref.at[site], sems.at[site]))
        copies[site].start()
    for copy in copies:
        copy.wait()
    msg_copy.wait()


def call(kernel, outs, scratch=(), in_specs=None, out_specs=None):
    specs = {}
    if in_specs is not None:
        specs["in_specs"] = in_specs
    if out_specs is not None:
        specs["out_specs"] = out_specs
    return pl.pallas_call(
        kernel,
        out_shape=[jax.ShapeDtypeStruct(shape, dtype) for shape, dtype in outs],
        scratch_shapes=list(scratch),
        compiler_params=pltpu.CompilerParams(vmem_limit_bytes=40 * 2**20),
        **specs,
    )


def swap_near(value):
    count = lax.axis_size("tile")
    return lax.ppermute(value, "tile", [(i, i ^ 1) for i in range(count)])


def swap_far(value):
    count = lax.axis_size("tile")
    pairs = []
    for group in range(2):
        for i in range(count):
            other = ((i + 1) ^ 1) - 1
            inner = 0 <= other < count
            target = group * count + other if inner else (1 - group) * count + i
            pairs.append((group * count + i, target))
    return lax.ppermute(value, ("group", "tile"), pairs)


def swap_side(value):
    return lax.ppermute(value, "group", [(0, 1), (1, 0)])


def exchange(near, far, side):
    return swap_near(near), swap_far(far), swap_side(side)


def per_device(site_tensors, msg_in):
    x = site_tensors.reshape(SITES, STATES, 2 * SQ, 128)
    x = x.transpose(0, 2, 1, 3).reshape(SITES, 4 * SQ, 128)
    x = pltpu.with_memory_space_constraint(x, pltpu.HBM)
    msg = pltpu.with_memory_space_constraint(msg_in[0], pltpu.HBM)
    flat = ((SITES, 4 * SQ, 128), bf16)
    tensor = ((SITES, STATES, SQ, SQ), bf16)
    messages = ((SITES, 4, SQ), f32)
    pack = ((D, WIDE), f32)
    packs = ((2 * D, WIDE), f32)
    in_hbm = [pl.BlockSpec(memory_space=pltpu.HBM)] * 2
    scratch = [
        pltpu.VMEM(*flat),
        pltpu.VMEM(*messages),
        pltpu.VMEM((SITES, 4 * SQ, 128), f32),
        pltpu.SemaphoreType.DMA((SITES + 1,)),
    ]
    forms, edges, own, *parts = call(
        first_kernel, [((2, *tensor[0]), bf16), pack, pack, pack, pack, pack], scratch, in_specs=in_hbm
    )(x, msg)
    received = exchange(*parts)
    ahead = call(
        ahead_kernel, [((2, STATES, SQ, SQ), f32), ((2, STATES, D, SQ), f32)]
    )(forms, edges, own, received[0])
    near, far, *parts = call(second_kernel, [packs] * 5)(forms, edges, own, *received, *ahead)
    received = exchange(*parts)
    spread = ((STATES, SITES, D, SQ), bf16)
    inner = ((STATES, 2, 2, D, SQ), bf16)
    early = call(early_kernel, [tensor, spread, inner])(forms, near, received[0])
    x, messages = call(last_kernel, [flat, messages], scratch, out_specs=in_hbm)(
        *early, edges, near, far, *received
    )
    x = x.reshape(SITES, 2 * SQ, STATES, 128).transpose(0, 2, 1, 3)
    return x.reshape(1, SITES, STATES, SQ * SQ), messages[None]


def solution(mesh):
    spec = P("tile", "group", None, None)
    return jax.shard_map(
        per_device, mesh=mesh, in_specs=(spec, spec), out_specs=(spec, spec), check_vma=False
    )
```

```python
import math

import jax
import jax.numpy as jnp
from jax import lax
from jax.experimental import pallas as pl
from jax.experimental.pallas import tpu as pltpu
from jax.sharding import PartitionSpec as P

D = 16
SQ = D * D
SITES = 3
STATES = 2
ITERS = 2
NS_STEPS = 6
UP, LEFT, DOWN, RIGHT = range(4)
LEGS = (UP, DOWN, LEFT, RIGHT)
SLOTS = 8
WIDE = SLOTS * D

epsilon = 1e-06
coupling_step = 0.5
field_step = 0.3
f32 = jnp.float32
bf16 = jnp.bfloat16


def iota(shape, dim):
    return lax.broadcasted_iota(jnp.int32, shape, dim)


def where_ones(condition):
    return jnp.where(condition, 1.0, 0.0).astype(bf16)


def minor(index):
    return index & (D - 1)


def major(index):
    return index >> 4


def selector(row_part, lane_part, lanes):
    return where_ones(row_part(iota((SQ, lanes), 0)) == lane_part(iota((SQ, lanes), 1)))


def dot(left, right):
    return jnp.dot(left, right, preferred_element_type=f32)


def dot_first(left, right):
    return lax.dot_general(left, right, (((0,), (0,)), ((), ())), preferred_element_type=f32)


def dot_split(left, right):
    high = left.astype(bf16)
    low = (left - high.astype(f32)).astype(bf16)
    return dot(high, right) + dot(low, right)


def kron(rep, tile):
    return (rep.astype(bf16)[:, None, :] * tile.astype(bf16)[None, :, :]).reshape(SQ, SQ)


def place():
    tile = lax.axis_index("tile")
    at_end = (tile == 0) | (tile == lax.axis_size("tile") - 1)
    return lax.axis_index("group") == 0, (tile & 1) == 0, at_end


def slot_of_lane():
    return major(iota((D, WIDE), 1))


def pack_of(blocks):
    slots = slot_of_lane()
    pack = jnp.zeros((D, WIDE), f32)
    for slot, block in enumerate(blocks):
        pack = jnp.where(slots == slot, block, pack)
    return pack


def packs_of(near, far, left, right):
    first_half, _, _ = place()
    side = jnp.where(first_half, right[2], left[0])
    inner = [right[0], right[1], left[1], left[2]]
    return pack_of(near + inner), pack_of(far + [side])


def rep(pack, slot):
    lane = iota((D, WIDE), 1)
    return jnp.concatenate(
        [
            jnp.take_along_axis(pack, slot * D + half * SLOTS + major(lane), axis=1)
            for half in range(2)
        ],
        axis=1,
    )


def tile(pack, slot):
    part = jnp.take_along_axis(pack, slot * D + minor(iota((D, WIDE), 1)), axis=1)
    return jnp.concatenate([part, part], axis=1)


def product(x_ref, form, site, s, weight):
    kept = dot(x_ref[form, site, s], weight).astype(bf16)
    return dot(kept, x_ref[1 - form, site, s])


def fold_minor(full, form):
    return jnp.sum(full.reshape(D, D, SQ) * form[None, :, :], axis=1)


def fold_major(full, form):
    return jnp.sum(full.reshape(D, D, SQ) * form[:, None, :], axis=0)


def site_parts(x_ref, site, up, left, down, right):
    parts = {}
    for form, m_rep, m_tile, k_rep, k_tile, leg_rep, leg_tile in (
        (0, up, left, down, right, UP, LEFT),
        (1, down, right, up, left, DOWN, RIGHT),
    ):
        weight = kron(k_rep, k_tile)
        full = product(x_ref, form, site, 0, weight) + product(x_ref, form, site, 1, weight)
        parts[leg_rep] = [fold_minor(full, m_tile)]
        parts[leg_tile] = [fold_major(full, m_rep)]
    return parts


def finish(parts, split_states):
    count = STATES if split_states else 1
    results = [{}, {}]
    for legs, pick in (
        ((UP, DOWN), selector(major, minor, WIDE)),
        ((LEFT, RIGHT), selector(minor, minor, WIDE)),
    ):
        rows = [parts[site][leg][s] for leg in legs for site in range(SITES) for s in range(count)]
        blocks = dot(jnp.concatenate(rows, axis=0).astype(bf16), pick).reshape(2, SITES, count, D, WIDE)
        for index, leg in enumerate(legs):
            block = blocks[index]
            summed = block[:, 0] + block[:, 1] if split_states else block[:, 0]
            mean = jnp.mean(summed * summed, axis=(1, 2), keepdims=True)
            inverse = 1.0 / jnp.sqrt(mean + epsilon)
            results[0][leg] = summed * inverse
            if split_states:
                results[1][leg] = (block[:, 0] - block[:, 1]) * inverse
    return results


def leg_rows(msg, leg):
    return jnp.concatenate([msg[site, leg : leg + 1] for site in range(SITES)], axis=0)


def first_kernel(
    x_ref, msg_ref, form_ref, edge_ref, own_ref, near_ref, far_ref, side_ref,
    x_buf, msg_buf, wide_ref, sems,
):
    copies = [
        pltpu.make_async_copy(x_ref.at[site], x_buf.at[site], sems.at[site])
        for site in range(SITES)
    ]
    msg_copy = pltpu.make_async_copy(msg_ref, msg_buf, sems.at[SITES])
    msg_copy.start()
    for copy in copies:
        copy.start()
    msg_copy.wait()
    msg = msg_buf[...]
    rows = jnp.concatenate([leg_rows(msg, leg) for leg in LEGS], axis=0)
    count = rows.shape[0]
    keep = iota((count, D, SQ), 1) == major(iota((count, D, SQ), 2))
    spread = jnp.broadcast_to(rows[:, None, :], (count, D, SQ))
    spread = jnp.where(keep, spread, 0.0).reshape(count * D, SQ)
    ends = dot(spread[: count // 2 * D].astype(bf16), selector(minor, major, SQ))
    sides = dot(spread[count // 2 * D :].astype(bf16), selector(minor, minor, SQ))
    ends, sides = (both.reshape(2, SITES, D, SQ) for both in (ends, sides))
    exact = dot_split(spread, selector(minor, minor, WIDE)).reshape(4, SITES, D, WIDE)
    first_half, even, _ = place()
    outer = jnp.where(first_half, exact[2, 0], exact[3, 2])
    edges = [jnp.where(even, exact[0, i], exact[1, i]) for i in range(SITES)]
    edge_ref[...] = pack_of(edges + [outer])
    parts = []
    for copy in copies:
        copy.wait()
    for site in range(SITES):
        wide_ref[site] = x_buf[site].astype(f32)
        for s in range(STATES):
            halves = [wide_ref[site, pl.ds(2 * half + s, SQ, stride=4), :] for half in range(2)]
            block = jnp.concatenate(halves, axis=1)
            form_ref[0, site, s] = block.astype(bf16)
            form_ref[1, site, s] = block.T.astype(bf16)
        parts.append(
            site_parts(form_ref, site, ends[0, site], sides[0, site], ends[1, site], sides[1, site])
        )
    out, _ = finish(parts, False)
    near = [jnp.where(even, out[DOWN][i], out[UP][i]) for i in range(SITES)]
    far = [jnp.where(even, out[UP][i], out[DOWN][i]) for i in range(SITES)]
    near, far = packs_of(near, far, out[LEFT], out[RIGHT])
    own_ref[...] = near
    near_ref[...] = near
    far_ref[...] = far
    side_ref[...] = far


def incoming_packs(near_own, edge, near_in, far_in, side_in):
    first_half, even, at_end = place()
    far = jnp.where(at_end, edge, far_in)
    up = jnp.where(even, far, near_in)
    down = jnp.where(even, near_in, far)
    left_end = jnp.where(first_half, edge, side_in)
    right_end = jnp.where(first_half, side_in, edge)
    return {
        UP: [(up, 0), (up, 1), (up, 2)],
        DOWN: [(down, 0), (down, 1), (down, 2)],
        LEFT: [(left_end, 3), (near_own, 3), (near_own, 4)],
        RIGHT: [(near_own, 5), (near_own, 6), (right_end, 3)],
    }


def site_forms(near, edge, own, far=None, side=None):
    first_half, even, _ = place()

    def pick(one, two):
        return jnp.where(first_half, one, two)

    sites = [1, pick(0, 2), pick(2, 0)]
    outer, near_side = tile(edge, 3), None if side is None else tile(side, 3)
    sides = [
        (tile(own, 3), tile(own, 6)),
        (pick(outer, tile(own, 4)), pick(tile(own, 5), outer)),
    ]
    if side is not None:
        sides.append((pick(tile(own, 4), near_side), pick(near_side, tile(own, 5))))
    forms = []
    for index, (left, right) in enumerate(sides):
        ends = []
        for pack in (near, far):
            if pack is None:
                ends.append(None)
            elif index == 0:
                ends.append(rep(pack, 1))
            else:
                zero, two = rep(pack, 0), rep(pack, 2)
                ends.append(pick(zero, two) if index == 1 else pick(two, zero))
        forms.append((sites[index], *ends, jnp.where(even, right, left), jnp.where(even, left, right)))
    return forms


def rounded(ref):
    return ref[...].astype(bf16).astype(f32)


def parity():
    return lax.axis_index("tile") & 1


def ahead_kernel(form_ref, edge_ref, near_own, near_in, full_ref, part_ref):
    form = parity()
    forms = site_forms(rounded(near_in), rounded(edge_ref), rounded(near_own))
    for index, (site, near, _, with_near, with_far) in enumerate(forms):
        weight = kron(near, with_near)
        for s in range(STATES):
            full = product(form_ref, form, site, s, weight)
            full_ref[index, s] = full
            part_ref[index, s] = fold_minor(full, with_far)


def second_kernel(
    form_ref, edge_ref, near_own, near_in, far_in, side_in, full_ref, part_ref,
    own_near_ref, own_far_ref, near_ref, far_ref, side_ref,
):
    first_half, even, at_end = place()
    form = parity()
    edge = rounded(edge_ref)
    far = jnp.where(at_end, edge, rounded(far_in))
    forms = site_forms(rounded(near_in), edge, rounded(near_own), far, rounded(side_in))
    parts = []
    for index, (site, near, far, with_near, with_far) in enumerate(forms):
        legs = {leg: [] for leg in LEGS}
        ahead, behind = kron(near, with_near), kron(far, with_far)
        for s in range(STATES):
            if index < 2:
                full, part = full_ref[index, s], part_ref[index, s]
            else:
                full = product(form_ref, form, site, s, ahead)
                part = fold_minor(full, with_far)
            legs[UP].append(part)
            legs[LEFT].append(fold_major(full, far))
            full = product(form_ref, 1 - form, site, s, behind)
            legs[DOWN].append(fold_minor(full, with_near))
            legs[RIGHT].append(fold_major(full, near))
        parts.append(legs)

    def by_site(values):
        middle, outer, inner = values
        return [jnp.where(first_half, outer, inner), middle, jnp.where(first_half, inner, outer)]

    for index, values in enumerate(finish(parts, True)):
        near, far, with_far, with_near = (
            by_site([values[leg][i] for i in range(SITES)]) for leg in (DOWN, UP, LEFT, RIGHT)
        )
        left = [jnp.where(even, with_far[i], with_near[i]) for i in range(SITES)]
        right = [jnp.where(even, with_near[i], with_far[i]) for i in range(SITES)]
        near, far = packs_of(near, far, left, right)
        part = slice(index * D, index * D + D)
        own_near_ref[part] = near
        own_far_ref[part] = far
        near_ref[part] = near
        far_ref[part] = far
        side_ref[part] = far


def sum_of(terms):
    while len(terms) > 1:
        terms = [sum(terms[i : i + 2][1:], terms[i]) for i in range(0, len(terms), 2)]
    return terms[0]


def columns_of(pack):
    base = iota((D, WIDE), 1) & -D
    return [jnp.take_along_axis(pack, base + k, axis=1) for k in range(D)]


def times(columns, right):
    return sum_of([columns[k] * right[k : k + 1, :] for k in range(D)])


def inverse_root(power, carried):
    for step in range(NS_STEPS):
        columns = columns_of(power)
        following = [1.5 * pack - 0.5 * times(columns, pack) for pack in carried]
        if step < NS_STEPS - 1:
            square = times(columns, power)
            power = 2.25 * power - 1.5 * square + 0.25 * times(columns, square)
        carried = following
    return carried


def bond_weights(both, both_twist, edge_lanes):
    weight_zero = math.cosh(coupling_step)
    weight_one = math.sinh(coupling_step)
    cross_weight = math.sqrt(weight_zero * weight_one)
    half_root = 1.0 / math.sqrt(2.0)
    top = ((weight_zero * both + cross_weight * both_twist) * half_root).astype(bf16).astype(f32)
    bottom = ((cross_weight * both_twist + weight_one * both) * half_root).astype(bf16).astype(f32)
    stacked = jnp.concatenate([top, bottom], axis=0).astype(bf16)
    inside = major(iota((WIDE, WIDE), 0)) == major(iota((WIDE, WIDE), 1))

    def packed(full):
        return jnp.sum(jnp.where(inside, full, 0.0).reshape(SLOTS, D, WIDE), axis=0)

    gram = packed(dot_first(stacked, stacked))
    squares = jnp.sum(top * top + bottom * bottom, axis=0, keepdims=True)
    squares = jnp.broadcast_to(squares, (D, WIDE))
    trace = dot_split(squares, where_ones(inside)) + epsilon
    identity = jnp.where(iota((D, WIDE), 0) == minor(iota((D, WIDE), 1)), 1.0, 0.0)
    spread = where_ones(iota((D, WIDE), 0) == minor(iota((D, WIDE), 1)))
    top_t, bottom_t = (packed(dot_first(half.astype(bf16), spread)) for half in (top, bottom))
    inverse, top_t, bottom_t = inverse_root(gram / trace, [identity, top_t, bottom_t])
    inverse = inverse.astype(bf16).astype(f32)
    root = 1.0 / jnp.sqrt(trace)
    results = []
    for q_top, q_bottom in (
        (times(columns_of(top), inverse), times(columns_of(bottom), inverse)),
        (top_t, bottom_t),
    ):
        first = math.sqrt(weight_zero) * (q_top * root)
        second = math.sqrt(weight_one) * (q_bottom * root)
        results.append(
            [
                jnp.where(edge_lanes, identity, weight).astype(bf16).astype(f32)
                for weight in (first + second, first - second)
            ]
        )
    return results


def early_kernel(form_ref, near_own, near_in, gated_ref, near_ref, inner_ref):
    _, even, _ = place()
    slots = slot_of_lane()
    other = (iota((D, WIDE), 1) + 2 * D) & (WIDE - 1)
    both = []
    for index in range(2):
        own = near_own[index * D : index * D + D]
        mate = jnp.take_along_axis(own, other, axis=1)
        mate = jnp.where(slots < 3, near_in[index * D : index * D + D], mate)
        both.append(jnp.where(slots < 5, own + mate, 0.0))
    grow, mix = math.cosh(field_step), math.sinh(field_step)
    for site in range(SITES):
        tensors = [form_ref[0, site, s].astype(f32) for s in range(STATES)]
        for s in range(STATES):
            gated_ref[site, s] = (grow * tensors[s] + mix * tensors[1 - s]).astype(bf16)
    plain, flipped = bond_weights(*both, slots < 0)
    for s in range(STATES):
        near = jnp.where(even, plain[s], flipped[s])
        for site in range(SITES):
            near_ref[s, site] = rep(near, site).astype(bf16)
        for index in range(2):
            inner_ref[s, 0, index] = tile(plain[s], 3 + index).astype(bf16)
            inner_ref[s, 1, index] = tile(flipped[s], 3 + index).astype(bf16)


def last_kernel(
    gated_ref, near_ref, inner_ref, edge_ref, near_own, far_own, near_in, far_in, side_in,
    x_ref, messages_ref, x_buf, msg_buf, wide_ref, sems,
):
    first_half, even, at_end = place()
    slots = slot_of_lane()
    where = incoming_packs(
        near_own[:D], edge_ref[...], near_in[:D], far_in[:D], side_in[:D]
    )
    own_row = iota((D, SQ), 0) == major(iota((D, SQ), 1))
    for leg in LEGS:
        for site in range(SITES):
            spread = jnp.where(own_row, tile(*where[leg][site]), 0.0)
            msg_buf[site, leg : leg + 1] = jnp.sum(spread, axis=0, keepdims=True)
    msg_copy = pltpu.make_async_copy(msg_buf, messages_ref, sems.at[SITES])
    msg_copy.start()
    both = []
    for index in range(2):
        part = slice(index * D, index * D + D)
        mate = jnp.where(slots < 3, far_in[part], side_in[part])
        both.append(jnp.where(slots < 4, far_own[part] + mate, 0.0))
    plain, flipped = bond_weights(*both, (slots < 3) & at_end)
    identity = where_ones(iota((D, SQ), 0) == minor(iota((D, SQ), 1)))
    factors = []
    for s in range(STATES):
        far_pack = jnp.where(even, flipped[s], plain[s])
        side = tile(jnp.where(first_half, plain[s], flipped[s]), 3).astype(bf16)
        far = [rep(far_pack, site).astype(bf16) for site in range(SITES)]
        near = [near_ref[s, site] for site in range(SITES)]
        ups = [jnp.where(even, far[i], near[i]) for i in range(SITES)]
        downs = [jnp.where(even, near[i], far[i]) for i in range(SITES)]
        lefts = [jnp.where(first_half, identity, side), inner_ref[s, 1, 0], inner_ref[s, 1, 1]]
        rights = [inner_ref[s, 0, 0], inner_ref[s, 0, 1], jnp.where(first_half, side, identity)]
        factors.append((ups, downs, lefts, rights))
    copies = []
    for site in range(SITES):
        for s in range(STATES):
            ups, downs, lefts, rights = factors[s]
            upper = kron(ups[site], lefts[site])
            lower = kron(downs[site], rights[site])
            gated = dot(upper, gated_ref[site, s]).astype(bf16)
            gated = dot(gated, lower)
            for half in range(2):
                lanes = gated[:, half * 128 : half * 128 + 128]
                wide_ref[site, pl.ds(2 * half + s, SQ, stride=4), :] = lanes
        x_buf[site] = wide_ref[site].astype(bf16)
        copies.append(pltpu.make_async_copy(x_buf.at[site], x_ref.at[site], sems.at[site]))
        copies[site].start()
    for copy in copies:
        copy.wait()
    msg_copy.wait()


def call(kernel, outs, scratch=(), in_specs=None, out_specs=None):
    specs = {}
    if in_specs is not None:
        specs["in_specs"] = in_specs
    if out_specs is not None:
        specs["out_specs"] = out_specs
    return pl.pallas_call(
        kernel,
        out_shape=[jax.ShapeDtypeStruct(shape, dtype) for shape, dtype in outs],
        scratch_shapes=list(scratch),
        compiler_params=pltpu.CompilerParams(vmem_limit_bytes=40 * 2**20),
        **specs,
    )


def swap_near(value):
    count = lax.axis_size("tile")
    return lax.ppermute(value, "tile", [(i, i ^ 1) for i in range(count)])


def swap_far(value):
    count = lax.axis_size("tile")
    pairs = []
    for group in range(2):
        for i in range(count):
            other = ((i + 1) ^ 1) - 1
            inner = 0 <= other < count
            target = group * count + other if inner else (1 - group) * count + i
            pairs.append((group * count + i, target))
    return lax.ppermute(value, ("group", "tile"), pairs)


def swap_side(value):
    return lax.ppermute(value, "group", [(0, 1), (1, 0)])


def exchange(near, far, side):
    return swap_near(near), swap_far(far), swap_side(side)


def per_device(site_tensors, msg_in):
    x = site_tensors.reshape(SITES, STATES, 2 * SQ, 128)
    x = x.transpose(0, 2, 1, 3).reshape(SITES, 4 * SQ, 128)
    x = pltpu.with_memory_space_constraint(x, pltpu.HBM)
    msg = pltpu.with_memory_space_constraint(msg_in[0], pltpu.HBM)
    flat = ((SITES, 4 * SQ, 128), bf16)
    tensor = ((SITES, STATES, SQ, SQ), bf16)
    messages = ((SITES, 4, SQ), f32)
    pack = ((D, WIDE), f32)
    packs = ((2 * D, WIDE), f32)
    in_hbm = [pl.BlockSpec(memory_space=pltpu.HBM)] * 2
    scratch = [
        pltpu.VMEM(*flat),
        pltpu.VMEM(*messages),
        pltpu.VMEM((SITES, 4 * SQ, 128), f32),
        pltpu.SemaphoreType.DMA((SITES + 1,)),
    ]
    forms, edges, own, *parts = call(
        first_kernel, [((2, *tensor[0]), bf16), pack, pack, pack, pack, pack], scratch, in_specs=in_hbm
    )(x, msg)
    received = exchange(*parts)
    ahead = call(
        ahead_kernel, [((2, STATES, SQ, SQ), f32), ((2, STATES, D, SQ), f32)]
    )(forms, edges, own, received[0])
    near, far, *parts = call(second_kernel, [packs] * 5)(forms, edges, own, *received, *ahead)
    received = exchange(*parts)
    spread = ((STATES, SITES, D, SQ), bf16)
    inner = ((STATES, 2, 2, D, SQ), bf16)
    early = call(early_kernel, [tensor, spread, inner])(forms, near, received[0])
    x, messages = call(last_kernel, [flat, messages], scratch, out_specs=in_hbm)(
        *early, edges, near, far, *received
    )
    x = x.reshape(SITES, 2 * SQ, STATES, 128).transpose(0, 2, 1, 3)
    return x.reshape(1, SITES, STATES, SQ * SQ), messages[None]


def solution(mesh):
    spec = P("tile", "group", None, None)
    return jax.shard_map(
        per_device, mesh=mesh, in_specs=(spec, spec), out_specs=(spec, spec), check_vma=False
    )
```

```python
import math

import jax
import jax.numpy as jnp
from jax import lax
from jax.experimental import pallas as pl
from jax.experimental.pallas import tpu as pltpu
from jax.sharding import PartitionSpec as P

D = 16
SQ = D * D
SITES = 3
STATES = 2
ITERS = 2
NS_STEPS = 6
UP, LEFT, DOWN, RIGHT = range(4)
LEGS = (UP, DOWN, LEFT, RIGHT)
SLOTS = 8
WIDE = SLOTS * D

epsilon = 1e-06
coupling_step = 0.5
field_step = 0.3
f32 = jnp.float32
bf16 = jnp.bfloat16


def iota(shape, dim):
    return lax.broadcasted_iota(jnp.int32, shape, dim)


def where_ones(condition):
    return jnp.where(condition, 1.0, 0.0).astype(bf16)


def minor(index):
    return index & (D - 1)


def major(index):
    return index >> 4


def selector(row_part, lane_part, lanes):
    return where_ones(row_part(iota((SQ, lanes), 0)) == lane_part(iota((SQ, lanes), 1)))


def dot(left, right):
    return jnp.dot(left, right, preferred_element_type=f32)


def dot_first(left, right):
    return lax.dot_general(left, right, (((0,), (0,)), ((), ())), preferred_element_type=f32)


def dot_split(left, right):
    high = left.astype(bf16)
    low = (left - high.astype(f32)).astype(bf16)
    return dot(high, right) + dot(low, right)


def kron(rep, tile):
    return (rep.astype(bf16)[:, None, :] * tile.astype(bf16)[None, :, :]).reshape(SQ, SQ)


def place():
    tile = lax.axis_index("tile")
    at_end = (tile == 0) | (tile == lax.axis_size("tile") - 1)
    return lax.axis_index("group") == 0, (tile & 1) == 0, at_end


def slot_of_lane():
    return major(iota((D, WIDE), 1))


def pack_of(blocks):
    slots = slot_of_lane()
    pack = jnp.zeros((D, WIDE), f32)
    for slot, block in enumerate(blocks):
        pack = jnp.where(slots == slot, block, pack)
    return pack


def packs_of(near, far, left, right):
    first_half, _, _ = place()
    side = jnp.where(first_half, right[2], left[0])
    inner = [right[0], right[1], left[1], left[2]]
    return pack_of(near + inner), pack_of(far + [side])


def rep(pack, slot):
    lane = iota((D, WIDE), 1)
    return jnp.concatenate(
        [
            jnp.take_along_axis(pack, slot * D + half * SLOTS + major(lane), axis=1)
            for half in range(2)
        ],
        axis=1,
    )


def tile(pack, slot):
    part = jnp.take_along_axis(pack, slot * D + minor(iota((D, WIDE), 1)), axis=1)
    return jnp.concatenate([part, part], axis=1)


def product(x_ref, form, site, s, weight):
    kept = dot(x_ref[form, site, s], weight).astype(bf16)
    return dot(kept, x_ref[1 - form, site, s])


def fold_minor(full, form):
    return jnp.sum(full.reshape(D, D, SQ) * form[None, :, :], axis=1)


def fold_major(full, form):
    return jnp.sum(full.reshape(D, D, SQ) * form[:, None, :], axis=0)


def site_parts(x_ref, site, up, left, down, right):
    parts = {}
    for form, m_rep, m_tile, k_rep, k_tile, leg_rep, leg_tile in (
        (0, up, left, down, right, UP, LEFT),
        (1, down, right, up, left, DOWN, RIGHT),
    ):
        weight = kron(k_rep, k_tile)
        kept = dot(x_ref[form, site].reshape(STATES * SQ, SQ), weight).astype(bf16)
        kept = jnp.concatenate([kept[:SQ], kept[SQ:]], axis=1)
        full = dot(kept, x_ref[1 - form, site].reshape(STATES * SQ, SQ))
        parts[leg_rep] = [fold_minor(full, m_tile)]
        parts[leg_tile] = [fold_major(full, m_rep)]
    return parts


def finish(parts, split_states):
    count = STATES if split_states else 1
    results = [{}, {}]
    for legs, pick in (
        ((UP, DOWN), selector(major, minor, WIDE)),
        ((LEFT, RIGHT), selector(minor, minor, WIDE)),
    ):
        rows = [parts[site][leg][s] for leg in legs for site in range(SITES) for s in range(count)]
        blocks = dot(jnp.concatenate(rows, axis=0).astype(bf16), pick).reshape(2, SITES, count, D, WIDE)
        for index, leg in enumerate(legs):
            block = blocks[index]
            summed = block[:, 0] + block[:, 1] if split_states else block[:, 0]
            mean = jnp.mean(summed * summed, axis=(1, 2), keepdims=True)
            inverse = 1.0 / jnp.sqrt(mean + epsilon)
            results[0][leg] = summed * inverse
            if split_states:
                results[1][leg] = (block[:, 0] - block[:, 1]) * inverse
    return results


def leg_rows(msg, leg):
    return jnp.concatenate([msg[site, leg : leg + 1] for site in range(SITES)], axis=0)


def first_kernel(
    x_ref, msg_ref, form_ref, edge_ref, own_ref, near_ref, far_ref, side_ref,
    x_buf, msg_buf, wide_ref, sems,
):
    copies = [
        pltpu.make_async_copy(x_ref.at[site], x_buf.at[site], sems.at[site])
        for site in range(SITES)
    ]
    msg_copy = pltpu.make_async_copy(msg_ref, msg_buf, sems.at[SITES])
    msg_copy.start()
    for copy in copies:
        copy.start()
    msg_copy.wait()
    msg = msg_buf[...]
    rows = jnp.concatenate([leg_rows(msg, leg) for leg in LEGS], axis=0)
    count = rows.shape[0]
    keep = iota((count, D, SQ), 1) == major(iota((count, D, SQ), 2))
    spread = jnp.broadcast_to(rows[:, None, :], (count, D, SQ))
    spread = jnp.where(keep, spread, 0.0).reshape(count * D, SQ)
    ends = dot(spread[: count // 2 * D].astype(bf16), selector(minor, major, SQ))
    sides = dot(spread[count // 2 * D :].astype(bf16), selector(minor, minor, SQ))
    ends, sides = (both.reshape(2, SITES, D, SQ) for both in (ends, sides))
    exact = dot_split(spread, selector(minor, minor, WIDE)).reshape(4, SITES, D, WIDE)
    first_half, even, _ = place()
    outer = jnp.where(first_half, exact[2, 0], exact[3, 2])
    edges = [jnp.where(even, exact[0, i], exact[1, i]) for i in range(SITES)]
    edge_ref[...] = pack_of(edges + [outer])
    parts = []
    for copy in copies:
        copy.wait()
    for site in range(SITES):
        wide_ref[site] = x_buf[site].astype(f32)
        for s in range(STATES):
            halves = [wide_ref[site, pl.ds(2 * half + s, SQ, stride=4), :] for half in range(2)]
            block = jnp.concatenate(halves, axis=1)
            form_ref[0, site, s] = block.astype(bf16)
            form_ref[1, site, s] = block.T.astype(bf16)
        parts.append(
            site_parts(form_ref, site, ends[0, site], sides[0, site], ends[1, site], sides[1, site])
        )
    out, _ = finish(parts, False)
    near = [jnp.where(even, out[DOWN][i], out[UP][i]) for i in range(SITES)]
    far = [jnp.where(even, out[UP][i], out[DOWN][i]) for i in range(SITES)]
    near, far = packs_of(near, far, out[LEFT], out[RIGHT])
    own_ref[...] = near
    near_ref[...] = near
    far_ref[...] = far
    side_ref[...] = far


def incoming_packs(near_own, edge, near_in, far_in, side_in):
    first_half, even, at_end = place()
    far = jnp.where(at_end, edge, far_in)
    up = jnp.where(even, far, near_in)
    down = jnp.where(even, near_in, far)
    left_end = jnp.where(first_half, edge, side_in)
    right_end = jnp.where(first_half, side_in, edge)
    return {
        UP: [(up, 0), (up, 1), (up, 2)],
        DOWN: [(down, 0), (down, 1), (down, 2)],
        LEFT: [(left_end, 3), (near_own, 3), (near_own, 4)],
        RIGHT: [(near_own, 5), (near_own, 6), (right_end, 3)],
    }


def site_forms(near, edge, own, far=None, side=None):
    first_half, even, _ = place()

    def pick(one, two):
        return jnp.where(first_half, one, two)

    sites = [1, pick(0, 2), pick(2, 0)]
    outer, near_side = tile(edge, 3), None if side is None else tile(side, 3)
    sides = [
        (tile(own, 3), tile(own, 6)),
        (pick(outer, tile(own, 4)), pick(tile(own, 5), outer)),
    ]
    if side is not None:
        sides.append((pick(tile(own, 4), near_side), pick(near_side, tile(own, 5))))
    forms = []
    for index, (left, right) in enumerate(sides):
        ends = []
        for pack in (near, far):
            if pack is None:
                ends.append(None)
            elif index == 0:
                ends.append(rep(pack, 1))
            else:
                zero, two = rep(pack, 0), rep(pack, 2)
                ends.append(pick(zero, two) if index == 1 else pick(two, zero))
        forms.append((sites[index], *ends, jnp.where(even, right, left), jnp.where(even, left, right)))
    return forms


def rounded(ref):
    return ref[...].astype(bf16).astype(f32)


def parity():
    return lax.axis_index("tile") & 1


def ahead_kernel(form_ref, edge_ref, near_own, near_in, full_ref, part_ref):
    form = parity()
    forms = site_forms(rounded(near_in), rounded(edge_ref), rounded(near_own))
    for index, (site, near, _, with_near, with_far) in enumerate(forms):
        weight = kron(near, with_near)
        for s in range(STATES):
            full = product(form_ref, form, site, s, weight)
            full_ref[index, s] = full
            part_ref[index, s] = fold_minor(full, with_far)


def second_kernel(
    form_ref, edge_ref, near_own, near_in, far_in, side_in, full_ref, part_ref,
    own_near_ref, own_far_ref, near_ref, far_ref, side_ref,
):
    first_half, even, at_end = place()
    form = parity()
    edge = rounded(edge_ref)
    far = jnp.where(at_end, edge, rounded(far_in))
    forms = site_forms(rounded(near_in), edge, rounded(near_own), far, rounded(side_in))
    parts = []
    for index, (site, near, far, with_near, with_far) in enumerate(forms):
        legs = {leg: [] for leg in LEGS}
        ahead, behind = kron(near, with_near), kron(far, with_far)
        for s in range(STATES):
            if index < 2:
                full, part = full_ref[index, s], part_ref[index, s]
            else:
                full = product(form_ref, form, site, s, ahead)
                part = fold_minor(full, with_far)
            legs[UP].append(part)
            legs[LEFT].append(fold_major(full, far))
            full = product(form_ref, 1 - form, site, s, behind)
            legs[DOWN].append(fold_minor(full, with_near))
            legs[RIGHT].append(fold_major(full, near))
        parts.append(legs)

    def by_site(values):
        middle, outer, inner = values
        return [jnp.where(first_half, outer, inner), middle, jnp.where(first_half, inner, outer)]

    for index, values in enumerate(finish(parts, True)):
        near, far, with_far, with_near = (
            by_site([values[leg][i] for i in range(SITES)]) for leg in (DOWN, UP, LEFT, RIGHT)
        )
        left = [jnp.where(even, with_far[i], with_near[i]) for i in range(SITES)]
        right = [jnp.where(even, with_near[i], with_far[i]) for i in range(SITES)]
        near, far = packs_of(near, far, left, right)
        part = slice(index * D, index * D + D)
        own_near_ref[part] = near
        own_far_ref[part] = far
        near_ref[part] = near
        far_ref[part] = far
        side_ref[part] = far


def sum_of(terms):
    while len(terms) > 1:
        terms = [sum(terms[i : i + 2][1:], terms[i]) for i in range(0, len(terms), 2)]
    return terms[0]


def columns_of(pack):
    base = iota((D, WIDE), 1) & -D
    return [jnp.take_along_axis(pack, base + k, axis=1) for k in range(D)]


def times(columns, right):
    return sum_of([columns[k] * right[k : k + 1, :] for k in range(D)])


def inverse_root(power, carried):
    for step in range(NS_STEPS):
        columns = columns_of(power)
        following = [1.5 * pack - 0.5 * times(columns, pack) for pack in carried]
        if step < NS_STEPS - 1:
            square = times(columns, power)
            power = 2.25 * power - 1.5 * square + 0.25 * times(columns, square)
        carried = following
    return carried


def bond_weights(both, both_twist, edge_lanes):
    weight_zero = math.cosh(coupling_step)
    weight_one = math.sinh(coupling_step)
    cross_weight = math.sqrt(weight_zero * weight_one)
    half_root = 1.0 / math.sqrt(2.0)
    top = ((weight_zero * both + cross_weight * both_twist) * half_root).astype(bf16).astype(f32)
    bottom = ((cross_weight * both_twist + weight_one * both) * half_root).astype(bf16).astype(f32)
    stacked = jnp.concatenate([top, bottom], axis=0).astype(bf16)
    inside = major(iota((WIDE, WIDE), 0)) == major(iota((WIDE, WIDE), 1))

    def packed(full):
        return jnp.sum(jnp.where(inside, full, 0.0).reshape(SLOTS, D, WIDE), axis=0)

    gram = packed(dot_first(stacked, stacked))
    squares = jnp.sum(top * top + bottom * bottom, axis=0, keepdims=True)
    squares = jnp.broadcast_to(squares, (D, WIDE))
    trace = dot_split(squares, where_ones(inside)) + epsilon
    identity = jnp.where(iota((D, WIDE), 0) == minor(iota((D, WIDE), 1)), 1.0, 0.0)
    spread = where_ones(iota((D, WIDE), 0) == minor(iota((D, WIDE), 1)))
    top_t, bottom_t = (packed(dot_first(half.astype(bf16), spread)) for half in (top, bottom))
    inverse, top_t, bottom_t = inverse_root(gram / trace, [identity, top_t, bottom_t])
    inverse = inverse.astype(bf16).astype(f32)
    root = 1.0 / jnp.sqrt(trace)
    results = []
    for q_top, q_bottom in (
        (times(columns_of(top), inverse), times(columns_of(bottom), inverse)),
        (top_t, bottom_t),
    ):
        first = math.sqrt(weight_zero) * (q_top * root)
        second = math.sqrt(weight_one) * (q_bottom * root)
        results.append(
            [
                jnp.where(edge_lanes, identity, weight).astype(bf16).astype(f32)
                for weight in (first + second, first - second)
            ]
        )
    return results


def early_kernel(form_ref, near_own, near_in, gated_ref, near_ref, inner_ref):
    _, even, _ = place()
    slots = slot_of_lane()
    other = (iota((D, WIDE), 1) + 2 * D) & (WIDE - 1)
    both = []
    for index in range(2):
        own = near_own[index * D : index * D + D]
        mate = jnp.take_along_axis(own, other, axis=1)
        mate = jnp.where(slots < 3, near_in[index * D : index * D + D], mate)
        both.append(jnp.where(slots < 5, own + mate, 0.0))
    grow, mix = math.cosh(field_step), math.sinh(field_step)
    for site in range(SITES):
        tensors = [form_ref[0, site, s].astype(f32) for s in range(STATES)]
        for s in range(STATES):
            gated_ref[site, s] = (grow * tensors[s] + mix * tensors[1 - s]).astype(bf16)
    plain, flipped = bond_weights(*both, slots < 0)
    for s in range(STATES):
        near = jnp.where(even, plain[s], flipped[s])
        for site in range(SITES):
            near_ref[s, site] = rep(near, site).astype(bf16)
        for index in range(2):
            inner_ref[s, 0, index] = tile(plain[s], 3 + index).astype(bf16)
            inner_ref[s, 1, index] = tile(flipped[s], 3 + index).astype(bf16)


def last_kernel(
    gated_ref, near_ref, inner_ref, edge_ref, near_own, far_own, near_in, far_in, side_in,
    x_ref, messages_ref, x_buf, msg_buf, wide_ref, sems,
):
    first_half, even, at_end = place()
    slots = slot_of_lane()
    where = incoming_packs(
        near_own[:D], edge_ref[...], near_in[:D], far_in[:D], side_in[:D]
    )
    own_row = iota((D, SQ), 0) == major(iota((D, SQ), 1))
    for leg in LEGS:
        for site in range(SITES):
            spread = jnp.where(own_row, tile(*where[leg][site]), 0.0)
            msg_buf[site, leg : leg + 1] = jnp.sum(spread, axis=0, keepdims=True)
    msg_copy = pltpu.make_async_copy(msg_buf, messages_ref, sems.at[SITES])
    msg_copy.start()
    both = []
    for index in range(2):
        part = slice(index * D, index * D + D)
        mate = jnp.where(slots < 3, far_in[part], side_in[part])
        both.append(jnp.where(slots < 4, far_own[part] + mate, 0.0))
    plain, flipped = bond_weights(*both, (slots < 3) & at_end)
    identity = where_ones(iota((D, SQ), 0) == minor(iota((D, SQ), 1)))
    factors = []
    for s in range(STATES):
        far_pack = jnp.where(even, flipped[s], plain[s])
        side = tile(jnp.where(first_half, plain[s], flipped[s]), 3).astype(bf16)
        far = [rep(far_pack, site).astype(bf16) for site in range(SITES)]
        near = [near_ref[s, site] for site in range(SITES)]
        ups = [jnp.where(even, far[i], near[i]) for i in range(SITES)]
        downs = [jnp.where(even, near[i], far[i]) for i in range(SITES)]
        lefts = [jnp.where(first_half, identity, side), inner_ref[s, 1, 0], inner_ref[s, 1, 1]]
        rights = [inner_ref[s, 0, 0], inner_ref[s, 0, 1], jnp.where(first_half, side, identity)]
        factors.append((ups, downs, lefts, rights))
    copies = []
    for site in range(SITES):
        for s in range(STATES):
            ups, downs, lefts, rights = factors[s]
            upper = kron(ups[site], lefts[site])
            lower = kron(downs[site], rights[site])
            gated = dot(upper, gated_ref[site, s]).astype(bf16)
            gated = dot(gated, lower)
            for half in range(2):
                lanes = gated[:, half * 128 : half * 128 + 128]
                wide_ref[site, pl.ds(2 * half + s, SQ, stride=4), :] = lanes
        x_buf[site] = wide_ref[site].astype(bf16)
        copies.append(pltpu.make_async_copy(x_buf.at[site], x_ref.at[site], sems.at[site]))
        copies[site].start()
    for copy in copies:
        copy.wait()
    msg_copy.wait()


def call(kernel, outs, scratch=(), in_specs=None, out_specs=None):
    specs = {}
    if in_specs is not None:
        specs["in_specs"] = in_specs
    if out_specs is not None:
        specs["out_specs"] = out_specs
    return pl.pallas_call(
        kernel,
        out_shape=[jax.ShapeDtypeStruct(shape, dtype) for shape, dtype in outs],
        scratch_shapes=list(scratch),
        compiler_params=pltpu.CompilerParams(vmem_limit_bytes=40 * 2**20),
        **specs,
    )


def swap_near(value):
    count = lax.axis_size("tile")
    return lax.ppermute(value, "tile", [(i, i ^ 1) for i in range(count)])


def swap_far(value):
    count = lax.axis_size("tile")
    pairs = []
    for group in range(2):
        for i in range(count):
            other = ((i + 1) ^ 1) - 1
            inner = 0 <= other < count
            target = group * count + other if inner else (1 - group) * count + i
            pairs.append((group * count + i, target))
    return lax.ppermute(value, ("group", "tile"), pairs)


def swap_side(value):
    return lax.ppermute(value, "group", [(0, 1), (1, 0)])


def exchange(near, far, side):
    return swap_near(near), swap_far(far), swap_side(side)


def per_device(site_tensors, msg_in):
    x = site_tensors.reshape(SITES, STATES, 2 * SQ, 128)
    x = x.transpose(0, 2, 1, 3).reshape(SITES, 4 * SQ, 128)
    x = pltpu.with_memory_space_constraint(x, pltpu.HBM)
    msg = pltpu.with_memory_space_constraint(msg_in[0], pltpu.HBM)
    flat = ((SITES, 4 * SQ, 128), bf16)
    tensor = ((SITES, STATES, SQ, SQ), bf16)
    messages = ((SITES, 4, SQ), f32)
    pack = ((D, WIDE), f32)
    packs = ((2 * D, WIDE), f32)
    in_hbm = [pl.BlockSpec(memory_space=pltpu.HBM)] * 2
    scratch = [
        pltpu.VMEM(*flat),
        pltpu.VMEM(*messages),
        pltpu.VMEM((SITES, 4 * SQ, 128), f32),
        pltpu.SemaphoreType.DMA((SITES + 1,)),
    ]
    forms, edges, own, *parts = call(
        first_kernel, [((2, *tensor[0]), bf16), pack, pack, pack, pack, pack], scratch, in_specs=in_hbm
    )(x, msg)
    received = exchange(*parts)
    ahead = call(
        ahead_kernel, [((2, STATES, SQ, SQ), f32), ((2, STATES, D, SQ), f32)]
    )(forms, edges, own, received[0])
    near, far, *parts = call(second_kernel, [packs] * 5)(forms, edges, own, *received, *ahead)
    received = exchange(*parts)
    spread = ((STATES, SITES, D, SQ), bf16)
    inner = ((STATES, 2, 2, D, SQ), bf16)
    early = call(early_kernel, [tensor, spread, inner])(forms, near, received[0])
    x, messages = call(last_kernel, [flat, messages], scratch, out_specs=in_hbm)(
        *early, edges, near, far, *received
    )
    x = x.reshape(SITES, 2 * SQ, STATES, 128).transpose(0, 2, 1, 3)
    return x.reshape(1, SITES, STATES, SQ * SQ), messages[None]


def solution(mesh):
    spec = P("tile", "group", None, None)
    return jax.shard_map(
        per_device, mesh=mesh, in_specs=(spec, spec), out_specs=(spec, spec), check_vma=False
    )
```

```python
import math

import jax
import jax.numpy as jnp
from jax import lax
from jax.experimental import pallas as pl
from jax.experimental.pallas import tpu as pltpu
from jax.sharding import PartitionSpec as P

D = 16
SQ = D * D
SITES = 3
STATES = 2
ITERS = 2
NS_STEPS = 6
UP, LEFT, DOWN, RIGHT = range(4)
LEGS = (UP, DOWN, LEFT, RIGHT)
SLOTS = 8
WIDE = SLOTS * D

epsilon = 1e-06
coupling_step = 0.5
field_step = 0.3
f32 = jnp.float32
bf16 = jnp.bfloat16


def iota(shape, dim):
    return lax.broadcasted_iota(jnp.int32, shape, dim)


def where_ones(condition):
    return jnp.where(condition, 1.0, 0.0).astype(bf16)


def minor(index):
    return index & (D - 1)


def major(index):
    return index >> 4


def selector(row_part, lane_part, lanes):
    return where_ones(row_part(iota((SQ, lanes), 0)) == lane_part(iota((SQ, lanes), 1)))


def dot(left, right):
    return jnp.dot(left, right, preferred_element_type=f32)


def dot_first(left, right):
    return lax.dot_general(left, right, (((0,), (0,)), ((), ())), preferred_element_type=f32)


def dot_split(left, right):
    high = left.astype(bf16)
    low = (left - high.astype(f32)).astype(bf16)
    return dot(high, right) + dot(low, right)


def kron(rep, tile):
    return (rep.astype(bf16)[:, None, :] * tile.astype(bf16)[None, :, :]).reshape(SQ, SQ)


def place():
    tile = lax.axis_index("tile")
    at_end = (tile == 0) | (tile == lax.axis_size("tile") - 1)
    return lax.axis_index("group") == 0, (tile & 1) == 0, at_end


def slot_of_lane():
    return major(iota((D, WIDE), 1))


def pack_of(blocks):
    slots = slot_of_lane()
    pack = jnp.zeros((D, WIDE), f32)
    for slot, block in enumerate(blocks):
        pack = jnp.where(slots == slot, block, pack)
    return pack


def packs_of(near, far, left, right):
    first_half, _, _ = place()
    side = jnp.where(first_half, right[2], left[0])
    inner = [right[0], right[1], left[1], left[2]]
    return pack_of(near + inner), pack_of(far + [side])


def rep(pack, slot):
    lane = iota((D, WIDE), 1)
    return jnp.concatenate(
        [
            jnp.take_along_axis(pack, slot * D + half * SLOTS + major(lane), axis=1)
            for half in range(2)
        ],
        axis=1,
    )


def tile(pack, slot):
    part = jnp.take_along_axis(pack, slot * D + minor(iota((D, WIDE), 1)), axis=1)
    return jnp.concatenate([part, part], axis=1)


def product(x_ref, form, site, s, weight):
    kept = dot(x_ref[form, site, s], weight).astype(bf16)
    return dot(kept, x_ref[1 - form, site, s])


def fold_minor(full, form):
    return jnp.sum(full.reshape(D, D, SQ) * form[None, :, :], axis=1)


def fold_major(full, form):
    return jnp.sum(full.reshape(D, D, SQ) * form[:, None, :], axis=0)


def site_parts(x_ref, site, up, left, down, right):
    parts = {}
    for form, m_rep, m_tile, k_rep, k_tile, leg_rep, leg_tile in (
        (0, up, left, down, right, UP, LEFT),
        (1, down, right, up, left, DOWN, RIGHT),
    ):
        weight = kron(k_rep, k_tile)
        kept = dot(x_ref[form, site].reshape(STATES * SQ, SQ), weight).astype(bf16)
        kept = jnp.concatenate([kept[:SQ], kept[SQ:]], axis=1)
        full = dot(kept, x_ref[1 - form, site].reshape(STATES * SQ, SQ))
        parts[leg_rep] = [fold_minor(full, m_tile)]
        parts[leg_tile] = [fold_major(full, m_rep)]
    return parts


def finish(parts, split_states):
    count = STATES if split_states else 1
    results = [{}, {}]
    for legs, pick in (
        ((UP, DOWN), selector(major, minor, WIDE)),
        ((LEFT, RIGHT), selector(minor, minor, WIDE)),
    ):
        rows = [parts[site][leg][s] for leg in legs for site in range(SITES) for s in range(count)]
        blocks = dot(jnp.concatenate(rows, axis=0).astype(bf16), pick).reshape(2, SITES, count, D, WIDE)
        for index, leg in enumerate(legs):
            block = blocks[index]
            summed = block[:, 0] + block[:, 1] if split_states else block[:, 0]
            mean = jnp.mean(summed * summed, axis=(1, 2), keepdims=True)
            inverse = 1.0 / jnp.sqrt(mean + epsilon)
            results[0][leg] = summed * inverse
            if split_states:
                results[1][leg] = (block[:, 0] - block[:, 1]) * inverse
    return results


def leg_rows(msg, leg):
    return jnp.concatenate([msg[site, leg : leg + 1] for site in range(SITES)], axis=0)


def first_kernel(
    x_ref, msg_ref, form_ref, edge_ref, own_ref, near_ref, far_ref, side_ref,
    x_buf, msg_buf, wide_ref, sems,
):
    copies = [
        pltpu.make_async_copy(x_ref.at[site], x_buf.at[site], sems.at[site])
        for site in range(SITES)
    ]
    msg_copy = pltpu.make_async_copy(msg_ref, msg_buf, sems.at[SITES])
    msg_copy.start()
    for copy in copies:
        copy.start()
    msg_copy.wait()
    msg = msg_buf[...]
    rows = jnp.concatenate([leg_rows(msg, leg) for leg in LEGS], axis=0)
    count = rows.shape[0]
    keep = iota((count, D, SQ), 1) == major(iota((count, D, SQ), 2))
    spread = jnp.broadcast_to(rows[:, None, :], (count, D, SQ))
    spread = jnp.where(keep, spread, 0.0).reshape(count * D, SQ)
    ends = dot(spread[: count // 2 * D].astype(bf16), selector(minor, major, SQ))
    sides = dot(spread[count // 2 * D :].astype(bf16), selector(minor, minor, SQ))
    ends, sides = (both.reshape(2, SITES, D, SQ) for both in (ends, sides))
    exact = dot_split(spread, selector(minor, minor, WIDE)).reshape(4, SITES, D, WIDE)
    first_half, even, _ = place()
    outer = jnp.where(first_half, exact[2, 0], exact[3, 2])
    edges = [jnp.where(even, exact[0, i], exact[1, i]) for i in range(SITES)]
    edge_ref[...] = pack_of(edges + [outer])
    parts = []
    for copy in copies:
        copy.wait()
    for site in range(SITES):
        wide_ref[site] = x_buf[site].astype(f32)
        for s in range(STATES):
            halves = [wide_ref[site, pl.ds(2 * half + s, SQ, stride=4), :] for half in range(2)]
            block = jnp.concatenate(halves, axis=1)
            form_ref[0, site, s] = block.astype(bf16)
            form_ref[1, site, s] = block.T.astype(bf16)
        parts.append(
            site_parts(form_ref, site, ends[0, site], sides[0, site], ends[1, site], sides[1, site])
        )
    out, _ = finish(parts, False)
    near = [jnp.where(even, out[DOWN][i], out[UP][i]) for i in range(SITES)]
    far = [jnp.where(even, out[UP][i], out[DOWN][i]) for i in range(SITES)]
    near, far = packs_of(near, far, out[LEFT], out[RIGHT])
    own_ref[...] = near
    near_ref[...] = near
    far_ref[...] = far
    side_ref[...] = far


def incoming_packs(near_own, edge, near_in, far_in, side_in):
    first_half, even, at_end = place()
    far = jnp.where(at_end, edge, far_in)
    up = jnp.where(even, far, near_in)
    down = jnp.where(even, near_in, far)
    left_end = jnp.where(first_half, edge, side_in)
    right_end = jnp.where(first_half, side_in, edge)
    return {
        UP: [(up, 0), (up, 1), (up, 2)],
        DOWN: [(down, 0), (down, 1), (down, 2)],
        LEFT: [(left_end, 3), (near_own, 3), (near_own, 4)],
        RIGHT: [(near_own, 5), (near_own, 6), (right_end, 3)],
    }


def site_forms(near, edge, own, far=None, side=None):
    first_half, even, _ = place()

    def pick(one, two):
        return jnp.where(first_half, one, two)

    sites = [1, pick(0, 2), pick(2, 0)]
    outer, near_side = tile(edge, 3), None if side is None else tile(side, 3)
    sides = [
        (tile(own, 3), tile(own, 6)),
        (pick(outer, tile(own, 4)), pick(tile(own, 5), outer)),
    ]
    if side is not None:
        sides.append((pick(tile(own, 4), near_side), pick(near_side, tile(own, 5))))
    forms = []
    for index, (left, right) in enumerate(sides):
        ends = []
        for pack in (near, far):
            if pack is None:
                ends.append(None)
            elif index == 0:
                ends.append(rep(pack, 1))
            else:
                zero, two = rep(pack, 0), rep(pack, 2)
                ends.append(pick(zero, two) if index == 1 else pick(two, zero))
        forms.append((sites[index], *ends, jnp.where(even, right, left), jnp.where(even, left, right)))
    return forms


def rounded(ref):
    return ref[...].astype(bf16).astype(f32)


def parity():
    return lax.axis_index("tile") & 1


def ahead_kernel(form_ref, edge_ref, near_own, near_in, full_ref, part_ref):
    form = parity()
    forms = site_forms(rounded(near_in), rounded(edge_ref), rounded(near_own))
    for index, (site, near, _, with_near, with_far) in enumerate(forms):
        weight = kron(near, with_near)
        for s in range(STATES):
            full = product(form_ref, form, site, s, weight)
            full_ref[index, s] = full
            part_ref[index, s] = fold_minor(full, with_far)


def second_kernel(
    form_ref, edge_ref, near_own, near_in, far_in, side_in, full_ref, part_ref,
    own_near_ref, own_far_ref, near_ref, far_ref, side_ref,
):
    first_half, even, at_end = place()
    form = parity()
    edge = rounded(edge_ref)
    far = jnp.where(at_end, edge, rounded(far_in))
    forms = site_forms(rounded(near_in), edge, rounded(near_own), far, rounded(side_in))
    parts = []
    for index, (site, near, far, with_near, with_far) in enumerate(forms):
        legs = {leg: [] for leg in LEGS}
        ahead, behind = kron(near, with_near), kron(far, with_far)
        for s in range(STATES):
            if index < 2:
                full, part = full_ref[index, s], part_ref[index, s]
            else:
                full = product(form_ref, form, site, s, ahead)
                part = fold_minor(full, with_far)
            legs[UP].append(part)
            legs[LEFT].append(fold_major(full, far))
            full = product(form_ref, 1 - form, site, s, behind)
            legs[DOWN].append(fold_minor(full, with_near))
            legs[RIGHT].append(fold_major(full, near))
        parts.append(legs)

    def by_site(values):
        middle, outer, inner = values
        return [jnp.where(first_half, outer, inner), middle, jnp.where(first_half, inner, outer)]

    for index, values in enumerate(finish(parts, True)):
        near, far, with_far, with_near = (
            by_site([values[leg][i] for i in range(SITES)]) for leg in (DOWN, UP, LEFT, RIGHT)
        )
        left = [jnp.where(even, with_far[i], with_near[i]) for i in range(SITES)]
        right = [jnp.where(even, with_near[i], with_far[i]) for i in range(SITES)]
        near, far = packs_of(near, far, left, right)
        part = slice(index * D, index * D + D)
        own_near_ref[part] = near
        own_far_ref[part] = far
        near_ref[part] = near
        far_ref[part] = far
        side_ref[part] = far


def sum_of(terms):
    while len(terms) > 1:
        terms = [sum(terms[i : i + 2][1:], terms[i]) for i in range(0, len(terms), 2)]
    return terms[0]


def columns_of(pack):
    base = iota((D, WIDE), 1) & -D
    return [jnp.take_along_axis(pack, base + k, axis=1) for k in range(D)]


def times(columns, right):
    return sum_of([columns[k] * right[k : k + 1, :] for k in range(D)])


def inverse_root(power, carried):
    for step in range(NS_STEPS):
        columns = columns_of(power)
        following = [1.5 * pack - 0.5 * times(columns, pack) for pack in carried]
        if step < NS_STEPS - 1:
            square = times(columns, power)
            power = 2.25 * power - 1.5 * square + 0.25 * times(columns, square)
        carried = following
    return carried


def bond_weights(both, both_twist, edge_lanes):
    weight_zero = math.cosh(coupling_step)
    weight_one = math.sinh(coupling_step)
    cross_weight = math.sqrt(weight_zero * weight_one)
    half_root = 1.0 / math.sqrt(2.0)
    top = ((weight_zero * both + cross_weight * both_twist) * half_root).astype(bf16).astype(f32)
    bottom = ((cross_weight * both_twist + weight_one * both) * half_root).astype(bf16).astype(f32)
    stacked = jnp.concatenate([top, bottom], axis=0).astype(bf16)
    inside = major(iota((WIDE, WIDE), 0)) == major(iota((WIDE, WIDE), 1))

    def packed(full):
        return jnp.sum(jnp.where(inside, full, 0.0).reshape(SLOTS, D, WIDE), axis=0)

    gram = packed(dot_first(stacked, stacked))
    squares = jnp.sum(top * top + bottom * bottom, axis=0, keepdims=True)
    squares = jnp.broadcast_to(squares, (D, WIDE))
    trace = dot_split(squares, where_ones(inside)) + epsilon
    identity = jnp.where(iota((D, WIDE), 0) == minor(iota((D, WIDE), 1)), 1.0, 0.0)
    spread = where_ones(iota((D, WIDE), 0) == minor(iota((D, WIDE), 1)))
    top_t, bottom_t = (packed(dot_first(half.astype(bf16), spread)) for half in (top, bottom))
    inverse, top_t, bottom_t = inverse_root(gram / trace, [identity, top_t, bottom_t])
    inverse = inverse.astype(bf16).astype(f32)
    root = 1.0 / jnp.sqrt(trace)
    results = []
    for q_top, q_bottom in (
        (times(columns_of(top), inverse), times(columns_of(bottom), inverse)),
        (top_t, bottom_t),
    ):
        first = math.sqrt(weight_zero) * (q_top * root)
        second = math.sqrt(weight_one) * (q_bottom * root)
        results.append(
            [
                jnp.where(edge_lanes, identity, weight).astype(bf16).astype(f32)
                for weight in (first + second, first - second)
            ]
        )
    return results


def early_kernel(form_ref, near_own, near_in, gated_ref, near_ref, inner_ref):
    _, even, _ = place()
    slots = slot_of_lane()
    other = (iota((D, WIDE), 1) + 2 * D) & (WIDE - 1)
    both = []
    for index in range(2):
        own = near_own[index * D : index * D + D]
        mate = jnp.take_along_axis(own, other, axis=1)
        mate = jnp.where(slots < 3, near_in[index * D : index * D + D], mate)
        both.append(jnp.where(slots < 5, own + mate, 0.0))
    grow, mix = math.cosh(field_step), math.sinh(field_step)
    for site in range(SITES):
        tensors = [form_ref[0, site, s].astype(f32) for s in range(STATES)]
        for s in range(STATES):
            gated_ref[site, s] = (grow * tensors[s] + mix * tensors[1 - s]).astype(bf16)
    plain, flipped = bond_weights(*both, slots < 0)
    for s in range(STATES):
        near = jnp.where(even, plain[s], flipped[s])
        for site in range(SITES):
            near_ref[s, site] = rep(near, site).astype(bf16)
        for index in range(2):
            inner_ref[s, 0, index] = tile(plain[s], 3 + index).astype(bf16)
            inner_ref[s, 1, index] = tile(flipped[s], 3 + index).astype(bf16)


def last_kernel(
    gated_ref, near_ref, inner_ref, edge_ref, near_own, far_own, near_in, far_in, side_in,
    x_ref, messages_ref, x_buf, msg_buf, wide_ref, sems,
):
    first_half, even, at_end = place()
    slots = slot_of_lane()
    where = incoming_packs(
        near_own[:D], edge_ref[...], near_in[:D], far_in[:D], side_in[:D]
    )
    own_row = iota((D, SQ), 0) == major(iota((D, SQ), 1))
    for leg in LEGS:
        for site in range(SITES):
            spread = jnp.where(own_row, tile(*where[leg][site]), 0.0)
            msg_buf[site, leg : leg + 1] = jnp.sum(spread, axis=0, keepdims=True)
    msg_copy = pltpu.make_async_copy(msg_buf, messages_ref, sems.at[SITES])
    msg_copy.start()
    both = []
    for index in range(2):
        part = slice(index * D, index * D + D)
        mate = jnp.where(slots < 3, far_in[part], side_in[part])
        both.append(jnp.where(slots < 4, far_own[part] + mate, 0.0))
    plain, flipped = bond_weights(*both, (slots < 3) & at_end)
    identity = where_ones(iota((D, SQ), 0) == minor(iota((D, SQ), 1)))
    factors = []
    for s in range(STATES):
        far_pack = jnp.where(even, flipped[s], plain[s])
        side = tile(jnp.where(first_half, plain[s], flipped[s]), 3).astype(bf16)
        far = [rep(far_pack, site).astype(bf16) for site in range(SITES)]
        near = [near_ref[s, site] for site in range(SITES)]
        ups = [jnp.where(even, far[i], near[i]) for i in range(SITES)]
        downs = [jnp.where(even, near[i], far[i]) for i in range(SITES)]
        lefts = [jnp.where(first_half, identity, side), inner_ref[s, 1, 0], inner_ref[s, 1, 1]]
        rights = [inner_ref[s, 0, 0], inner_ref[s, 0, 1], jnp.where(first_half, side, identity)]
        factors.append((ups, downs, lefts, rights))
    copies = []
    for site in range(SITES):
        for s in range(STATES):
            ups, downs, lefts, rights = factors[s]
            upper = kron(ups[site], lefts[site])
            lower = kron(downs[site], rights[site])
            gated = dot(gated_ref[site, s], lower).astype(bf16)
            gated = dot(upper, gated)
            for half in range(2):
                lanes = gated[:, half * 128 : half * 128 + 128]
                wide_ref[site, pl.ds(2 * half + s, SQ, stride=4), :] = lanes
        x_buf[site] = wide_ref[site].astype(bf16)
        copies.append(pltpu.make_async_copy(x_buf.at[site], x_ref.at[site], sems.at[site]))
        copies[site].start()
    for copy in copies:
        copy.wait()
    msg_copy.wait()


def call(kernel, outs, scratch=(), in_specs=None, out_specs=None):
    specs = {}
    if in_specs is not None:
        specs["in_specs"] = in_specs
    if out_specs is not None:
        specs["out_specs"] = out_specs
    return pl.pallas_call(
        kernel,
        out_shape=[jax.ShapeDtypeStruct(shape, dtype) for shape, dtype in outs],
        scratch_shapes=list(scratch),
        compiler_params=pltpu.CompilerParams(vmem_limit_bytes=40 * 2**20),
        **specs,
    )


def swap_near(value):
    count = lax.axis_size("tile")
    return lax.ppermute(value, "tile", [(i, i ^ 1) for i in range(count)])


def swap_far(value):
    count = lax.axis_size("tile")
    pairs = []
    for group in range(2):
        for i in range(count):
            other = ((i + 1) ^ 1) - 1
            inner = 0 <= other < count
            target = group * count + other if inner else (1 - group) * count + i
            pairs.append((group * count + i, target))
    return lax.ppermute(value, ("group", "tile"), pairs)


def swap_side(value):
    return lax.ppermute(value, "group", [(0, 1), (1, 0)])


def exchange(near, far, side):
    return swap_near(near), swap_far(far), swap_side(side)


def per_device(site_tensors, msg_in):
    x = site_tensors.reshape(SITES, STATES, 2 * SQ, 128)
    x = x.transpose(0, 2, 1, 3).reshape(SITES, 4 * SQ, 128)
    x = pltpu.with_memory_space_constraint(x, pltpu.HBM)
    msg = pltpu.with_memory_space_constraint(msg_in[0], pltpu.HBM)
    flat = ((SITES, 4 * SQ, 128), bf16)
    tensor = ((SITES, STATES, SQ, SQ), bf16)
    messages = ((SITES, 4, SQ), f32)
    pack = ((D, WIDE), f32)
    packs = ((2 * D, WIDE), f32)
    in_hbm = [pl.BlockSpec(memory_space=pltpu.HBM)] * 2
    scratch = [
        pltpu.VMEM(*flat),
        pltpu.VMEM(*messages),
        pltpu.VMEM((SITES, 4 * SQ, 128), f32),
        pltpu.SemaphoreType.DMA((SITES + 1,)),
    ]
    forms, edges, own, *parts = call(
        first_kernel, [((2, *tensor[0]), bf16), pack, pack, pack, pack, pack], scratch, in_specs=in_hbm
    )(x, msg)
    received = exchange(*parts)
    ahead = call(
        ahead_kernel, [((2, STATES, SQ, SQ), f32), ((2, STATES, D, SQ), f32)]
    )(forms, edges, own, received[0])
    near, far, *parts = call(second_kernel, [packs] * 5)(forms, edges, own, *received, *ahead)
    received = exchange(*parts)
    spread = ((STATES, SITES, D, SQ), bf16)
    inner = ((STATES, 2, 2, D, SQ), bf16)
    early = call(early_kernel, [tensor, spread, inner])(forms, near, received[0])
    x, messages = call(last_kernel, [flat, messages], scratch, out_specs=in_hbm)(
        *early, edges, near, far, *received
    )
    x = x.reshape(SITES, 2 * SQ, STATES, 128).transpose(0, 2, 1, 3)
    return x.reshape(1, SITES, STATES, SQ * SQ), messages[None]


def solution(mesh):
    spec = P("tile", "group", None, None)
    return jax.shard_map(
        per_device, mesh=mesh, in_specs=(spec, spec), out_specs=(spec, spec), check_vma=False
    )
```
